512 devices in a mesh: step: 2 (over x_hi), grp: 16 (over y, core), ctx: 16 (over z, x_lo).
Axes of the slice: x: 4 (x_hi: 2, x_lo: 2; x = x_hi * 2 + x_lo), y: 8, z: 8, core: 2. Of those that a mesh axis runs over, the one named last changes fastest.
Arguments:
- queries: bfloat16 [2, 32768, 2560], P('step', ('grp', 'ctx')), parts along dimension 1, may hold values from -22.5 to 22.5
- keys: bfloat16 [2, 32768, 2560], P('step', ('grp', 'ctx')), parts along dimension 1, may hold values from -22.5 to 22.5
- values: bfloat16 [2, 32768, 2560], P('step', ('grp', 'ctx')), parts along dimension 1, may hold values from -6 to 6
- cotangent: bfloat16 [32768, 2560], P(('grp', 'ctx')), parts along dimension 0, may hold values from -6 to 6
- merge_sizes: int32 [32768], P(('grp', 'ctx')), parts along dimension 0, may hold values from 1 to 4
- router_logits: float32 [20], replicated, may hold values from -2 to 2
- gate_plan: int32 [20], replicated, may hold values 0 or 1
Outputs:
- grad_queries: bfloat16 [2, 32768, 2560], P('step', ('grp', 'ctx')), parts along dimension 1
- grad_keys: bfloat16 [2, 32768, 2560], P('step', ('grp', 'ctx')), parts along dimension 1
- grad_values: bfloat16 [2, 32768, 2560], P('step', ('grp', 'ctx')), parts along dimension 1
- router_grad: float32 [320], P('grp'), parts along dimension 0
The draws below stay inside these ranges and needn't reach their ends.
There are 16 independent parts, one for each index of `grp`. The reference program is written for one: setup_inputs(seed, part) draws one part's arguments, and reference() takes and returns one part's arrays. A program takes and returns all parts, laid end to end along the dimension named above; an argument that names none is the same for every part. Nothing has to cross between parts.
All inputs are finite; a program needn't handle non-finite values.
Results may differ from the reference program's by a relative error of at most 0.009.
Values may be sent and summed in bfloat16 or wider, within the bound.
A program may use at most 128 MiB of HBM per device.

```python
import math
import jax
import jax.numpy as jnp
from jax import lax

H = 20
DH = 128
QB = 4
TOKENS = 2048
F = 2560


def draw_queries(key, part):
    key = jax.random.fold_in(key, 11)
    return jnp.clip(jax.random.normal(key, (2, TOKENS, F), jnp.float32), -6.0, 6.0).astype(jnp.bfloat16)


def draw_keys(key, part):
    key = jax.random.fold_in(key, 23)
    return jnp.clip(jax.random.normal(key, (2, TOKENS, F), jnp.float32), -6.0, 6.0).astype(jnp.bfloat16)


def place_ends(result, own_key, smallest, largest):
    shape = result.shape
    spot = [jax.random.randint(jax.random.fold_in(own_key, axis), (), 0, shape[axis]) for axis in range(len(shape))]
    result = result.at[tuple(spot)].set(smallest)
    longest = shape.index(max(shape))
    spot[longest] = (spot[longest] + 1) % shape[longest]
    return result.at[tuple(spot)].set(largest)


def shard_levels(stream_key, shape, cuts, low, largest):
    factor_of = 1.0
    for axis_at, blocks in cuts:
        steps = jax.random.uniform(jax.random.fold_in(jax.random.fold_in(stream_key, 6), axis_at), (blocks,), jnp.float32, low / len(cuts), largest / len(cuts))
        factor_of = factor_of * jnp.repeat(jnp.exp(steps), shape[axis_at] // blocks).reshape((-1,) + (1,) * (len(shape) - 1 - axis_at))
    return factor_of


def gaussian(own_key, shape, deviation, most, cuts=(), kind=jnp.bfloat16):
    entries = deviation * jax.random.normal(own_key, shape, jnp.float32)
    if cuts:
        entries = entries * shard_levels(own_key, shape, cuts, -0.22, 0.18)
    return jnp.clip(entries, -most, most).astype(kind)


def setup_inputs(seed: int = 0, part: int = 0) -> dict:
    key_list = jax.random.split(jax.random.key(seed), 8)
    own_keys = jax.random.split(jax.random.fold_in(key_list[7], part), 8)
    queries = draw_queries(jax.random.fold_in(jax.random.fold_in(key_list[7], part), 71), part)
    keys = draw_keys(jax.random.fold_in(jax.random.fold_in(key_list[7], part), 71), part)
    values = gaussian(own_keys[2], (2, TOKENS, F), 1.0, 6.0, ((0, 2), (1, 16)))
    cotangent = gaussian(own_keys[3], (TOKENS, F), 1.0, 6.0, ((0, 16),))
    merge_sizes = place_ends(jax.random.randint(own_keys[4], (TOKENS,), 1, 5), jax.random.fold_in(own_keys[4], 1), 1, 4).astype(jnp.int32)
    router_logits = jnp.clip(jax.random.uniform(key_list[5], (H,), jnp.float32, -2.0, 2.0), -2.0, 2.0)
    gate_plan = place_ends((jax.random.randint(key_list[6], (H,), 0, 4) < 3).astype(jnp.int32), jax.random.fold_in(key_list[6], 1), 0, 1)
    return {"queries": queries, "keys": keys, "values": values, "cotangent": cotangent, "merge_sizes": merge_sizes, "router_logits": router_logits, "gate_plan": gate_plan}


def block_grads(q_block, k_head, v_head, g_block, bias, coef):
    score_scale = DH ** (-0.5)
    scores = lax.dot_general(q_block, k_head, (((1,), (1,)), ((), ())), preferred_element_type=jnp.float32) * score_scale + bias[None, :]
    shifted = scores - lax.optimization_barrier(jnp.max(scores, axis=1, keepdims=True))
    expon = jnp.exp(shifted)
    probs = expon / lax.optimization_barrier(jnp.sum(expon, axis=1, keepdims=True))
    probs_b = probs.astype(jnp.bfloat16)
    outer = lax.dot_general(g_block, v_head, (((1,), (1,)), ((), ())), preferred_element_type=jnp.float32)
    rowdot = lax.optimization_barrier(jnp.sum(probs * outer, axis=1))
    dscore = (coef * probs * (outer - rowdot[:, None])).astype(jnp.bfloat16)
    dq_rows = jnp.dot(dscore, k_head, preferred_element_type=jnp.float32) * score_scale
    dk_part = lax.dot_general(dscore, q_block, (((0,), (0,)), ((), ())), preferred_element_type=jnp.float32) * score_scale
    dv_part = coef * lax.dot_general(probs_b, g_block, (((0,), (0,)), ((), ())), preferred_element_type=jnp.float32)
    return (dq_rows, dk_part, dv_part, jnp.sum(rowdot))

def split_heads(array):
    return array.reshape(TOKENS, H, DH).transpose(1, 0, 2)

def merge_heads(array):
    return array.transpose(1, 0, 2).reshape(TOKENS, H * DH).astype(jnp.bfloat16)

def reference(queries, keys, values, cotangent, merge_sizes, router_logits, gate_plan):
    beta = jnp.where(gate_plan == 1, jax.nn.sigmoid(router_logits), jnp.float32(1.0))
    bias = jnp.log(merge_sizes.astype(jnp.float32))
    block_rows = TOKENS // QB
    grad_split = split_heads(cotangent)
    results = []
    sums = []
    for section in range(2):
        coef_all = beta if section == 1 else 1.0 - beta

        def per_head(items):
            q_head, k_head, v_head, g_head, coef = items

            def per_block(carry, block):
                dk_sum, dv_sum, r_sum = carry
                start = (block * block_rows).astype(jnp.int32)
                q_block = lax.dynamic_slice_in_dim(q_head, start, block_rows, 0)
                g_block = lax.dynamic_slice_in_dim(g_head, start, block_rows, 0)
                dq_rows, dk_part, dv_part, r_part = block_grads(q_block, k_head, v_head, g_block, bias, coef)
                return ((dk_sum + dk_part, dv_sum + dv_part, r_sum + r_part), dq_rows)
            start_carry = (jnp.zeros((TOKENS, DH), jnp.float32), jnp.zeros((TOKENS, DH), jnp.float32), jnp.float32(0.0))
            (dk_sum, dv_sum, r_sum), dq_blocks = lax.scan(per_block, start_carry, jnp.arange(QB, dtype=jnp.int32))
            return (dq_blocks.reshape(TOKENS, DH), dk_sum, dv_sum, r_sum)
        dq_heads, dk_heads, dv_heads, r_heads = lax.map(per_head, (split_heads(queries[section]), split_heads(keys[section]), split_heads(values[section]), grad_split, coef_all))
        results.append((merge_heads(dq_heads), merge_heads(dk_heads), merge_heads(dv_heads)))
        sums.append(r_heads)
    grad_queries = jnp.stack([results[0][0], results[1][0]])
    grad_keys = jnp.stack([results[0][1], results[1][1]])
    grad_values = jnp.stack([results[0][2], results[1][2]])
    router_grad = beta * (1.0 - beta) * (sums[1] - sums[0]) / math.sqrt(TOKENS)
    return (grad_queries, grad_keys, grad_values, router_grad)
```

```python
import functools
import math

import jax
import jax.numpy as jnp
from jax import lax
from jax.experimental import pallas as pl
from jax.experimental.pallas import tpu as pltpu
from jax.sharding import PartitionSpec as P

MESH = pl.DeviceIdType.MESH
DH = 128
NDEV = 16
ROWS = 128
TOK = NDEV * ROWS
HEADS = 20
BQ = 512
CK = 256
UNITS = TOK // BQ
SCALE = DH ** -0.5
NT = (((1,), (1,)), ((), ()))


def owner_of(h, core):
    early = h < 8
    last = h >= 16
    i = jnp.where(early, h, h - 8)
    z = 2 * (i // 2) + jnp.where(early, core, 1 - core)
    x = i % 2
    j = h - 16
    z = jnp.where(last, 2 * j + core, z)
    x = jnp.where(last, j % 2, x)
    return z * 2 + x


def kernel(
    coef_ref, q_ref, k_ref, v_ref, g_ref, ms_ref,
    dq_out, dk_out, dv_out, r_out,
    qb, kb, vb, gb, msb, kx, kt, s_buf, o_buf, ds_buf, dk_acc, dv_acc,
    dqs, dks, dvs, rmine, rother, rb,
    in_send, in_recv, ms_send, ms_recv, out_send, out_recv,
    rp_send, rp_recv, rb_send, rb_recv,
):
    me = lax.axis_index("ctx")
    step = lax.axis_index("step")
    core = lax.axis_index("grp") % 2
    z = me // 2
    x = me % 2
    early = (z + core) % 2 == 0
    double = jnp.logical_and(early, (z // 2) % 2 == x)
    first_head = jnp.where(early, 0, 8) + (z // 2) * 2 + x
    second_head = 16 + z // 2
    n_slots = jnp.where(double, 2, 1)

    barrier = pltpu.get_barrier_semaphore()

    def greet(j, _):
        pl.semaphore_signal(
            barrier, inc=1, device_id={"ctx": (me + j) % NDEV}, device_id_type=MESH
        )
        return 0

    lax.fori_loop(1, NDEV, greet, 0)
    pl.semaphore_signal(barrier, inc=1, device_id={"step": 1 - step}, device_id_type=MESH)
    pl.semaphore_wait(barrier, NDEV)

    my_rows = pl.ds(pl.multiple_of(me * ROWS, ROWS), ROWS)

    def ms_copy(j):
        return pltpu.make_async_remote_copy(
            src_ref=ms_ref, dst_ref=msb.at[me], send_sem=ms_send, recv_sem=ms_recv,
            device_id={"ctx": (me + j) % NDEV}, device_id_type=MESH,
        )

    def send_ms(j, _):
        ms_copy(j).start()
        return 0

    lax.fori_loop(1, NDEV, send_ms, 0)
    pltpu.make_async_copy(ms_ref, msb.at[me], ms_recv).start()

    def send_head(h):
        owner = owner_of(h, core)
        slot = h // 16
        cols = pl.ds(pl.multiple_of(h * DH, DH), DH)
        pairs = (
            (k_ref.at[0, :, cols], kb.at[slot, my_rows], 0),
            (v_ref.at[0, :, cols], vb.at[slot, my_rows], 1),
            (q_ref.at[0, :, cols], qb.at[slot, my_rows], 2),
            (g_ref.at[:, cols], gb.at[slot, my_rows], 3),
        )

        @pl.when(owner == me)
        def _():
            for src, dst, a in pairs:
                pltpu.make_async_copy(src, dst, in_recv.at[slot, a]).start()

        @pl.when(owner != me)
        def _():
            for src, dst, a in pairs:
                pltpu.make_async_remote_copy(
                    src_ref=src, dst_ref=dst, send_sem=in_send.at[h],
                    recv_sem=in_recv.at[slot, a],
                    device_id={"ctx": owner}, device_id_type=MESH,
                ).start()

    def send_early(j, _):
        send_head((me // 2 + j) % 8)
        return 0

    def send_late(j, _):
        send_head(8 + (me + j) % 12)
        return 0

    lax.fori_loop(0, 8, send_early, 0)
    lax.fori_loop(0, 12, send_late, 0)

    pltpu.make_async_copy(msb, msb, ms_recv).wait()
    lane = lax.broadcasted_iota(jnp.int32, (ROWS, ROWS), 1)
    row = lax.broadcasted_iota(jnp.int32, (ROWS, ROWS), 0)

    def extend(t, _):
        logs = jnp.log(msb[t].astype(jnp.float32)) * (1.0 / SCALE)
        spread = jnp.where(lane == row, jnp.broadcast_to(logs, (ROWS, ROWS)), 0.0)
        column = jnp.sum(spread, axis=1, keepdims=True)
        hi = column.astype(jnp.bfloat16).astype(jnp.float32)
        rest = column - hi
        mid = rest.astype(jnp.bfloat16).astype(jnp.float32)
        low = rest - mid
        ext = jnp.where(lane == 0, hi, jnp.where(lane == 1, mid, jnp.where(lane == 2, low, 0.0)))
        kx[pl.ds(pl.multiple_of(t * ROWS, ROWS), ROWS), :] = ext.astype(jnp.bfloat16)
        return 0

    lax.fori_loop(0, NDEV, extend, 0)

    ones = jnp.ones((BQ, DH), jnp.bfloat16)

    def do_slot(slot, _):
        h = jnp.where(slot == 0, first_head, second_head)
        coef = coef_ref[h]
        cols = pl.ds(pl.multiple_of(h * DH, DH), DH)
        for a, buf in enumerate((kb, vb, qb, gb)):
            pltpu.make_async_copy(buf.at[slot], buf.at[slot], in_recv.at[slot, a]).wait()

        def transpose_keys(t, _):
            rows = pl.ds(pl.multiple_of(t * ROWS, ROWS), ROWS)
            kt[:, rows] = kb[slot, rows, :].astype(jnp.float32).T.astype(jnp.bfloat16)
            dk_acc[rows, :] = jnp.zeros((ROWS, DH), jnp.float32)
            dv_acc[rows, :] = jnp.zeros((ROWS, DH), jnp.float32)
            return 0

        lax.fori_loop(0, NDEV, transpose_keys, 0)

        def send_rows(src_buf, dst_out, a, t):
            rows = pl.ds(pl.multiple_of(t * ROWS, ROWS), ROWS)
            src = src_buf.at[slot, rows]
            dst = dst_out.at[0, :, cols]

            @pl.when(t == me)
            def _():
                pltpu.make_async_copy(src, dst, out_recv.at[a]).start()

            @pl.when(t != me)
            def _():
                pltpu.make_async_remote_copy(
                    src_ref=src, dst_ref=dst, send_sem=out_send.at[slot, a],
                    recv_sem=out_recv.at[a], device_id={"ctx": t}, device_id_type=MESH,
                ).start()

        def unit(b, r_sum):
            q_rows = pl.ds(pl.multiple_of(b * BQ, BQ), BQ)
            q_ext = jnp.concatenate([qb[slot, q_rows, :], ones], axis=1)

            def pass1(c, top):
                rows = pl.ds(pl.multiple_of(c * CK, CK), CK)
                k_ext = jnp.concatenate([kb[slot, rows, :], kx[rows, :]], axis=1)
                s = lax.dot_general(k_ext, q_ext, NT, preferred_element_type=jnp.float32)
                s_buf[rows, :] = s
                return jnp.maximum(top, jnp.max(s.reshape(CK // 8, 8, BQ), axis=0))

            top = lax.fori_loop(
                0, TOK // CK, pass1, jnp.full((8, BQ), -jnp.inf, jnp.float32)
            )
            top = jnp.max(top, axis=0, keepdims=True)

            def pass2(c, carry):
                l_sum, rd_sum = carry
                rows = pl.ds(pl.multiple_of(c * CK, CK), CK)
                o = lax.dot_general(
                    vb[slot, rows, :], gb[slot, q_rows, :], NT,
                    preferred_element_type=jnp.float32,
                )
                e = jnp.exp2((s_buf[rows, :] - top) * (SCALE * math.log2(math.e)))
                s_buf[rows, :] = e
                o_buf[rows, :] = o
                l_sum = l_sum + jnp.sum(e.reshape(CK // 8, 8, BQ), axis=0)
                rd_sum = rd_sum + jnp.sum((e * o).reshape(CK // 8, 8, BQ), axis=0)
                return (l_sum, rd_sum)

            zero = jnp.zeros((8, BQ), jnp.float32)
            l_sum, rd_sum = lax.fori_loop(0, TOK // CK, pass2, (zero, zero))
            inv = 1.0 / jnp.sum(l_sum, axis=0, keepdims=True)
            rd = jnp.sum(rd_sum, axis=0, keepdims=True) * inv
            for i in range(BQ // DH):
                r_sum = r_sum + rd[:, i * DH:(i + 1) * DH]
            inv_col = jnp.concatenate(
                [
                    jnp.broadcast_to(inv[:, i * DH:(i + 1) * DH], (DH, DH)).T
                    for i in range(BQ // DH)
                ],
                axis=0,
            ) * coef
            g_scaled = (gb[slot, q_rows, :].astype(jnp.float32) * inv_col).astype(jnp.bfloat16)
            inv_col = inv_col * SCALE
            q_scaled = (qb[slot, q_rows, :].astype(jnp.float32) * inv_col).astype(jnp.bfloat16)

            def pass3(c, _):
                rows = pl.ds(pl.multiple_of(c * CK, CK), CK)
                e = s_buf[rows, :]
                ds = (e * (o_buf[rows, :] - rd)).astype(jnp.bfloat16)
                ds_buf[rows, :] = ds
                dv_acc[rows, :] += jnp.dot(
                    e.astype(jnp.bfloat16), g_scaled, preferred_element_type=jnp.float32
                )
                dk_acc[rows, :] += jnp.dot(ds, q_scaled, preferred_element_type=jnp.float32)
                return 0

            lax.fori_loop(0, TOK // CK, pass3, 0)
            dqt = jnp.dot(kt[...], ds_buf[...], preferred_element_type=jnp.float32)
            dqs[slot, q_rows, :] = (dqt.T * inv_col).astype(jnp.bfloat16)
            for i in range(BQ // ROWS):
                send_rows(dqs, dq_out, 0, b * (BQ // ROWS) + i)
            return r_sum

        r_sum = lax.fori_loop(0, UNITS, unit, jnp.zeros((1, DH), jnp.float32))

        def finish(t, _):
            rows = pl.ds(pl.multiple_of(t * ROWS, ROWS), ROWS)
            dks[slot, rows, :] = dk_acc[rows, :].astype(jnp.bfloat16)
            dvs[slot, rows, :] = dv_acc[rows, :].astype(jnp.bfloat16)
            send_rows(dks, dk_out, 1, t)
            send_rows(dvs, dv_out, 2, t)
            return 0

        lax.fori_loop(0, NDEV, finish, 0)
        rmine[slot] = jnp.broadcast_to(jnp.sum(r_sum, axis=1, keepdims=True), (8, DH))
        partner_copy(slot).start()
        return 0

    def partner_copy(slot):
        return pltpu.make_async_remote_copy(
            src_ref=rmine.at[slot], dst_ref=rother.at[slot],
            send_sem=rp_send.at[slot], recv_sem=rp_recv.at[slot],
            device_id={"step": 1 - step}, device_id_type=MESH,
        )

    lax.fori_loop(0, n_slots, do_slot, 0)

    sign = jnp.where(step == 1, 1.0, -1.0).astype(jnp.float32)

    def spread_router(slot, _):
        h = jnp.where(slot == 0, first_head, second_head)
        partner_copy(slot).wait()
        rmine[slot] = (rmine[slot] - rother[slot]) * sign

        def send(j, _):
            pltpu.make_async_remote_copy(
                src_ref=rmine.at[slot], dst_ref=rb.at[h],
                send_sem=rb_send.at[slot], recv_sem=rb_recv,
                device_id={"ctx": (me + j) % NDEV}, device_id_type=MESH,
            ).start()
            return 0

        lax.fori_loop(1, NDEV, send, 0)
        pltpu.make_async_copy(rmine.at[slot], rb.at[h], rb_recv).start()
        return 0

    lax.fori_loop(0, n_slots, spread_router, 0)

    pltpu.make_async_copy(msb.at[pl.ds(0, NDEV - 1)], msb.at[pl.ds(0, NDEV - 1)], ms_send).wait()

    def sent_head(h, _):
        @pl.when(owner_of(h, core) != me)
        def _():
            pltpu.make_async_copy(
                kb.at[0, pl.ds(0, 4 * ROWS)], kb.at[0, pl.ds(0, 4 * ROWS)], in_send.at[h]
            ).wait()

        return 0

    lax.fori_loop(0, HEADS, sent_head, 0)

    def sent_slot(slot, _):
        for a, buf in enumerate((dqs, dks, dvs)):
            part = buf.at[slot, pl.ds(0, TOK - ROWS)]
            pltpu.make_async_copy(part, part, out_send.at[slot, a]).wait()
        part = rb.at[pl.ds(0, NDEV - 1)]
        pltpu.make_async_copy(part, part, rb_send.at[slot]).wait()
        return 0

    lax.fori_loop(0, n_slots, sent_slot, 0)

    pltpu.make_async_copy(rb, rb, rb_recv).wait()
    r_out[...] = rb[...]
    for a, out in enumerate((dq_out, dk_out, dv_out)):
        pltpu.make_async_copy(out, out, out_recv.at[a]).wait()


def body(queries, keys, values, cotangent, merge_sizes, router_logits, gate_plan):
    step = lax.axis_index("step")
    beta = jnp.where(gate_plan == 1, jax.nn.sigmoid(router_logits), jnp.float32(1.0))
    coef = jnp.where(step == 1, beta, 1.0 - beta)
    shape = queries.shape
    bf16, f32 = jnp.bfloat16, jnp.float32
    anywhere = pl.BlockSpec(memory_space=pl.ANY)
    dma = pltpu.SemaphoreType.DMA
    dq, dk, dv, r = pl.pallas_call(
        kernel,
        out_shape=[
            jax.ShapeDtypeStruct(shape, bf16),
            jax.ShapeDtypeStruct(shape, bf16),
            jax.ShapeDtypeStruct(shape, bf16),
            jax.ShapeDtypeStruct((HEADS, 8, DH), f32),
        ],
        in_specs=[pl.BlockSpec(memory_space=pltpu.SMEM)] + [anywhere] * 5,
        out_specs=[anywhere] * 3 + [pl.BlockSpec(memory_space=pltpu.VMEM)],
        scratch_shapes=[
            pltpu.VMEM((2, TOK, DH), bf16),
            pltpu.VMEM((2, TOK, DH), bf16),
            pltpu.VMEM((2, TOK, DH), bf16),
            pltpu.VMEM((2, TOK, DH), bf16),
            pltpu.VMEM((NDEV, 1, ROWS), jnp.int32),
            pltpu.VMEM((TOK, DH), bf16),
            pltpu.VMEM((DH, TOK), bf16),
            pltpu.VMEM((TOK, BQ), f32),
            pltpu.VMEM((TOK, BQ), f32),
            pltpu.VMEM((TOK, BQ), bf16),
            pltpu.VMEM((TOK, DH), f32),
            pltpu.VMEM((TOK, DH), f32),
            pltpu.VMEM((2, TOK, DH), bf16),
            pltpu.VMEM((2, TOK, DH), bf16),
            pltpu.VMEM((2, TOK, DH), bf16),
            pltpu.VMEM((2, 8, DH), f32),
            pltpu.VMEM((2, 8, DH), f32),
            pltpu.VMEM((HEADS, 8, DH), f32),
            dma((HEADS,)),
            dma((2, 4)),
            dma, dma,
            dma((2, 3)),
            dma((3,)),
            dma((2,)), dma((2,)),
            dma((2,)), dma,
        ],
        compiler_params=pltpu.CompilerParams(
            collective_id=0, has_side_effects=True, vmem_limit_bytes=48 * 1024 * 1024
        ),
        cost_estimate=pl.CostEstimate(
            flops=7_000_000_000, bytes_accessed=5_000_000, transcendentals=5_000_000
        ),
    )(coef, queries, keys, values, cotangent, merge_sizes.reshape(1, ROWS))
    router_grad = beta * (1.0 - beta) * r[:, 0, 0] / math.sqrt(TOK)
    return (dq, dk, dv, router_grad)


def solution(mesh):
    return jax.shard_map(
        body,
        mesh=mesh,
        in_specs=(
            P("step", ("grp", "ctx"), None),
            P("step", ("grp", "ctx"), None),
            P("step", ("grp", "ctx"), None),
            P(("grp", "ctx"), None),
            P(("grp", "ctx")),
            P(),
            P(),
        ),
        out_specs=(
            P("step", ("grp", "ctx"), None),
            P("step", ("grp", "ctx"), None),
            P("step", ("grp", "ctx"), None),
            P("grp"),
        ),
        check_vma=False,
    )
```

```python
import functools
import math

import jax
import jax.numpy as jnp
from jax import lax
from jax.experimental import pallas as pl
from jax.experimental.pallas import tpu as pltpu
from jax.sharding import PartitionSpec as P

MESH = pl.DeviceIdType.MESH
DH = 128
NDEV = 16
ROWS = 128
TOK = NDEV * ROWS
HEADS = 20
BQ = 512
CK = 1024
HALF = ROWS // 2
UNITS = TOK // BQ
SCALE = DH ** -0.5
NT = (((1,), (1,)), ((), ()))


def owner_of(h, core):
    early = h < 8
    last = h >= 16
    i = jnp.where(early, h, h - 8)
    z = 2 * (i // 2) + jnp.where(early, core, 1 - core)
    x = i % 2
    j = h - 16
    z = jnp.where(last, 2 * j + core, z)
    x = jnp.where(last, core, x)
    return z * 2 + x


def kernel(
    logit_ref, gate_ref, q_ref, k_ref, v_ref, g_ref, ms_ref,
    dq_out, dk_out, dv_out, r_out,
    qb, kb, vb, gb, msb, kx, kt, s_buf, o_buf, ds_buf, dk_acc, dv_acc,
    dqs, dks, dvs, rmine, rb, rrow, rother,
    in_send, in_recv, gf_send, gf_recv, ms_send, ms_recv, out_send, out_recv,
    rp_send, rp_recv, rb_send, rb_recv,
):
    me = lax.axis_index("ctx")
    step = lax.axis_index("step")
    core = lax.axis_index("grp") % 2
    z = me // 2
    x = me % 2
    early = (z + core) % 2 == 0
    double = jnp.logical_and(early, x == core)
    first_head = jnp.where(early, 0, 8) + (z // 2) * 2 + x
    second_head = 16 + z // 2
    n_slots = jnp.where(double, 2, 1)

    barrier = pltpu.get_barrier_semaphore()

    def greet(j, _):
        pl.semaphore_signal(
            barrier, inc=1, device_id={"ctx": (me + j) % NDEV}, device_id_type=MESH
        )
        return 0

    lax.fori_loop(1, NDEV, greet, 0)
    pl.semaphore_signal(barrier, inc=1, device_id={"step": 1 - step}, device_id_type=MESH)
    pl.semaphore_wait(barrier, NDEV)

    my_rows = pl.ds(pl.multiple_of(me * ROWS, ROWS), ROWS)

    def ms_copy(j):
        return pltpu.make_async_remote_copy(
            src_ref=ms_ref, dst_ref=msb.at[me], send_sem=ms_send, recv_sem=ms_recv,
            device_id={"ctx": (me + j) % NDEV}, device_id_type=MESH,
        )

    def send_ms(j, _):
        ms_copy(j).start()
        return 0

    lax.fori_loop(1, NDEV, send_ms, 0)
    pltpu.make_async_copy(ms_ref, msb.at[me], ms_recv).start()

    def send_pairs(h, pairs):
        owner = owner_of(h, core)

        @pl.when(owner == me)
        def _():
            for src, dst, sem in pairs:
                pltpu.make_async_copy(src, dst, sem).start()

        @pl.when(owner != me)
        def _():
            for src, dst, sem in pairs:
                pltpu.make_async_remote_copy(
                    src_ref=src, dst_ref=dst, send_sem=in_send.at[h], recv_sem=sem,
                    device_id={"ctx": owner}, device_id_type=MESH,
                ).start()

    def columns(h):
        return pl.ds(pl.multiple_of(h * DH, DH), DH)

    def send_g(h):
        slot = h // 16
        rows = pl.ds(pl.multiple_of(step * HALF, HALF), HALF)
        send_pairs(h, ((g_ref.at[rows, columns(h)], gb.at[slot, me, step], in_recv.at[slot, 3]),))

    def send_qkv(h):
        slot = h // 16
        cols = columns(h)
        send_pairs(h, (
            (k_ref.at[0, :, cols], kb.at[slot, my_rows], in_recv.at[slot, 0]),
            (v_ref.at[0, :, cols], vb.at[slot, my_rows], in_recv.at[slot, 1]),
            (q_ref.at[0, :, cols], qb.at[slot, my_rows], in_recv.at[slot, 2]),
        ))

    def loop(send, first, count, start):
        def one(j, _):
            send(first + (start + j) % count)
            return 0

        lax.fori_loop(0, count, one, 0)

    loop(send_g, 0, 8, z)
    loop(send_g, 16, 4, z // 2)
    loop(send_qkv, 0, 8, z)
    loop(send_g, 8, 8, z)
    loop(send_qkv, 16, 4, z // 2)
    loop(send_qkv, 8, 8, z)

    def forward_g(slot):
        return pltpu.make_async_remote_copy(
            src_ref=gb.at[slot, :, step], dst_ref=gb.at[slot, :, step],
            send_sem=gf_send.at[slot], recv_sem=gf_recv.at[slot],
            device_id={"step": 1 - step}, device_id_type=MESH,
        )

    pltpu.make_async_copy(msb, msb, ms_recv).wait()
    lane = lax.broadcasted_iota(jnp.int32, (ROWS, ROWS), 1)
    row = lax.broadcasted_iota(jnp.int32, (ROWS, ROWS), 0)

    def extend(t, _):
        logs = jnp.log(msb[t].astype(jnp.float32)) * (1.0 / SCALE)
        spread = jnp.where(lane == row, jnp.broadcast_to(logs, (ROWS, ROWS)), 0.0)
        column = jnp.sum(spread, axis=1, keepdims=True)
        hi = column.astype(jnp.bfloat16).astype(jnp.float32)
        rest = column - hi
        mid = rest.astype(jnp.bfloat16).astype(jnp.float32)
        low = rest - mid
        ext = jnp.where(lane == 0, hi, jnp.where(lane == 1, mid, jnp.where(lane == 2, low, 0.0)))
        kx[pl.ds(pl.multiple_of(t * ROWS, ROWS), ROWS), :] = ext.astype(jnp.bfloat16)
        return 0

    lax.fori_loop(0, NDEV, extend, 0)

    def pass_g_on(slot, _):
        half = gb.at[slot, :, step]
        pltpu.make_async_copy(half, half, in_recv.at[slot, 3]).wait()
        forward_g(slot).start()
        return 0

    lax.fori_loop(0, n_slots, pass_g_on, 0)

    beta = jnp.where(gate_ref[...] == 1, jax.nn.sigmoid(logit_ref[...]), 1.0)
    coef_row = jnp.where(step == 1, beta, 1.0 - beta)
    head_lane = lax.broadcasted_iota(jnp.int32, (1, HEADS), 1)
    ones = jnp.ones((BQ, DH), jnp.bfloat16)

    def do_slot(slot, _):
        h = jnp.where(slot == 0, first_head, second_head)
        coef = jnp.sum(jnp.where(head_lane == h, coef_row, 0.0), axis=1, keepdims=True)
        cols = columns(h)
        for a, buf in enumerate((kb, vb, qb)):
            pltpu.make_async_copy(buf.at[slot], buf.at[slot], in_recv.at[slot, a]).wait()
        forward_g(slot).wait_recv()

        def transpose_keys(t, _):
            rows = pl.ds(pl.multiple_of(t * ROWS, ROWS), ROWS)
            kt[:, rows] = kb[slot, rows, :].astype(jnp.float32).T.astype(jnp.bfloat16)
            dk_acc[rows, :] = jnp.zeros((ROWS, DH), jnp.float32)
            dv_acc[rows, :] = jnp.zeros((ROWS, DH), jnp.float32)
            return 0

        lax.fori_loop(0, NDEV, transpose_keys, 0)

        def send_rows(src_buf, dst_out, a, t):
            rows = pl.ds(pl.multiple_of(t * ROWS, ROWS), ROWS)
            src = src_buf.at[slot, rows]
            dst = dst_out.at[0, :, cols]

            @pl.when(t == me)
            def _():
                pltpu.make_async_copy(src, dst, out_recv.at[a]).start()

            @pl.when(t != me)
            def _():
                pltpu.make_async_remote_copy(
                    src_ref=src, dst_ref=dst, send_sem=out_send.at[slot, a],
                    recv_sem=out_recv.at[a], device_id={"ctx": t}, device_id_type=MESH,
                ).start()

        def unit(b, r_sum):
            q_rows = pl.ds(pl.multiple_of(b * BQ, BQ), BQ)
            g_blk = gb[slot, pl.ds(b * (BQ // ROWS), BQ // ROWS)].reshape(BQ, DH)
            q_ext = jnp.concatenate([qb[slot, q_rows, :], ones], axis=1)

            def pass1(c, top):
                rows = pl.ds(pl.multiple_of(c * CK, CK), CK)
                k_ext = jnp.concatenate([kb[slot, rows, :], kx[rows, :]], axis=1)
                s = lax.dot_general(k_ext, q_ext, NT, preferred_element_type=jnp.float32)
                s_buf[rows, :] = s
                return jnp.maximum(top, jnp.max(s.reshape(CK // 8, 8, BQ), axis=0))

            top = lax.fori_loop(
                0, TOK // CK, pass1, jnp.full((8, BQ), -jnp.inf, jnp.float32)
            )
            top = jnp.max(top, axis=0, keepdims=True)

            def pass2(c, carry):
                l_sum, rd_sum = carry
                rows = pl.ds(pl.multiple_of(c * CK, CK), CK)
                o = lax.dot_general(
                    vb[slot, rows, :], g_blk, NT,
                    preferred_element_type=jnp.float32,
                )
                e = jnp.exp2((s_buf[rows, :] - top) * (SCALE * math.log2(math.e)))
                s_buf[rows, :] = e
                o_buf[rows, :] = o
                l_sum = l_sum + jnp.sum(e.reshape(CK // 8, 8, BQ), axis=0)
                rd_sum = rd_sum + jnp.sum((e * o).reshape(CK // 8, 8, BQ), axis=0)
                return (l_sum, rd_sum)

            zero = jnp.zeros((8, BQ), jnp.float32)
            l_sum, rd_sum = lax.fori_loop(0, TOK // CK, pass2, (zero, zero))
            inv = 1.0 / jnp.sum(l_sum, axis=0, keepdims=True)
            rd = jnp.sum(rd_sum, axis=0, keepdims=True) * inv
            for i in range(BQ // DH):
                r_sum = r_sum + rd[:, i * DH:(i + 1) * DH]

            @pl.when(b == UNITS - 1)
            def _():
                rmine[slot] = r_sum

                def send_r(j, _):
                    pltpu.make_async_remote_copy(
                        src_ref=rmine.at[slot], dst_ref=rb.at[h],
                        send_sem=rb_send.at[slot], recv_sem=rb_recv,
                        device_id={"ctx": (me + j) % NDEV}, device_id_type=MESH,
                    ).start()
                    return 0

                lax.fori_loop(1, NDEV, send_r, 0)
                pltpu.make_async_copy(rmine.at[slot], rb.at[h], rb_recv).start()

            inv = inv * coef
            inv_col = jnp.concatenate(
                [
                    jnp.broadcast_to(inv[:, i * DH:(i + 1) * DH], (DH, DH)).T
                    for i in range(BQ // DH)
                ],
                axis=0,
            )
            g_scaled = (g_blk.astype(jnp.float32) * inv_col).astype(jnp.bfloat16)
            inv_col = inv_col * SCALE
            q_scaled = (qb[slot, q_rows, :].astype(jnp.float32) * inv_col).astype(jnp.bfloat16)

            def pass3(c, _):
                rows = pl.ds(pl.multiple_of(c * CK, CK), CK)
                e = s_buf[rows, :]
                ds = (e * (o_buf[rows, :] - rd)).astype(jnp.bfloat16)
                ds_buf[rows, :] = ds
                dv_acc[rows, :] += jnp.dot(
                    e.astype(jnp.bfloat16), g_scaled, preferred_element_type=jnp.float32
                )
                dk_acc[rows, :] += jnp.dot(ds, q_scaled, preferred_element_type=jnp.float32)
                return 0

            def finish(t, _):
                rows = pl.ds(pl.multiple_of(t * ROWS, ROWS), ROWS)
                dks[slot, rows, :] = dk_acc[rows, :].astype(jnp.bfloat16)
                dvs[slot, rows, :] = dv_acc[rows, :].astype(jnp.bfloat16)
                send_rows(dks, dk_out, 1, t)
                send_rows(dvs, dv_out, 2, t)
                return 0

            def pass3_send(c, _):
                pass3(c, 0)

                @pl.when(b == UNITS - 1)
                def _():
                    lax.fori_loop(c * (CK // ROWS), (c + 1) * (CK // ROWS), finish, 0)

                return 0

            lax.fori_loop(0, TOK // CK, pass3_send, 0)
            dqt = jnp.dot(kt[...], ds_buf[...], preferred_element_type=jnp.float32)
            dqs[slot, q_rows, :] = (dqt.T * inv_col).astype(jnp.bfloat16)

            def send_dq(i, _):
                send_rows(dqs, dq_out, 0, b * (BQ // ROWS) + i)
                return 0

            lax.fori_loop(0, BQ // ROWS, send_dq, 0)
            return r_sum

        lax.fori_loop(0, UNITS, unit, jnp.zeros((1, DH), jnp.float32))
        return 0

    lax.fori_loop(0, n_slots, do_slot, 0)

    pltpu.make_async_copy(rb, rb, rb_recv).wait()
    sums = jnp.sum(rb[...], axis=2)
    diagonal = (
        lax.broadcasted_iota(jnp.int32, (HEADS, DH), 0)
        == lax.broadcasted_iota(jnp.int32, (HEADS, DH), 1)
    )
    rrow[...] = jnp.sum(jnp.where(diagonal, sums, 0.0), axis=0, keepdims=True)
    to_partner = pltpu.make_async_remote_copy(
        src_ref=rrow, dst_ref=rother, send_sem=rp_send, recv_sem=rp_recv,
        device_id={"step": 1 - step}, device_id_type=MESH,
    )
    to_partner.start()

    pltpu.make_async_copy(msb.at[pl.ds(0, NDEV - 1)], msb.at[pl.ds(0, NDEV - 1)], ms_send).wait()

    sent = kb.at[0, pl.ds(0, 3 * ROWS + HALF)]

    def sent_head(h, _):
        @pl.when(owner_of(h, core) != me)
        def _():
            pltpu.make_async_copy(
                sent, sent, in_send.at[h]
            ).wait()

        return 0

    lax.fori_loop(0, HEADS, sent_head, 0)

    def sent_slot(slot, _):
        for a, buf in enumerate((dqs, dks, dvs)):
            part = buf.at[slot, pl.ds(0, TOK - ROWS)]
            pltpu.make_async_copy(part, part, out_send.at[slot, a]).wait()
        part = rb.at[pl.ds(0, NDEV - 1)]
        pltpu.make_async_copy(part, part, rb_send.at[slot]).wait()
        forward_g(slot).wait_send()
        return 0

    lax.fori_loop(0, n_slots, sent_slot, 0)

    to_partner.wait()
    sign = jnp.where(step == 1, 1.0, -1.0).astype(jnp.float32)
    total = (rrow[...] - rother[...]) * sign
    r_out[...] = beta * (1.0 - beta) * total[:, :HEADS] * (1.0 / math.sqrt(TOK))
    for a, out in enumerate((dq_out, dk_out, dv_out)):
        pltpu.make_async_copy(out, out, out_recv.at[a]).wait()


def hand_over(
    dq_in, dk_in, dv_in, r_in, dq_out, dk_out, dv_out, r_out, held, r_held, sems_in, sems_out,
):
    into, onward = [pltpu.make_async_copy(r_in, r_held, sems_in.at[0])], []
    onward.append(pltpu.make_async_copy(r_held, r_out, sems_out.at[0]))
    for a, (src, dst) in enumerate(((dq_in, dq_out), (dk_in, dk_out), (dv_in, dv_out))):
        for i in range(2):
            rows = pl.ds(i * HALF, HALF)
            n = 1 + 2 * a + i
            into.append(pltpu.make_async_copy(src.at[0, rows], held.at[a, rows], sems_in.at[n]))
            onward.append(pltpu.make_async_copy(held.at[a, rows], dst.at[0, rows], sems_out.at[n]))
    for copy in into:
        copy.start()
    for copy, after in zip(into, onward):
        copy.wait()
        after.start()
    for copy in onward:
        copy.wait()


def body(queries, keys, values, cotangent, merge_sizes, router_logits, gate_plan):
    shape = queries.shape
    bf16, f32 = jnp.bfloat16, jnp.float32
    anywhere = pl.BlockSpec(memory_space=pl.ANY)
    whole = pl.BlockSpec(memory_space=pltpu.VMEM)
    dma = pltpu.SemaphoreType.DMA
    dq, dk, dv, r = pl.pallas_call(
        kernel,
        out_shape=[
            jax.ShapeDtypeStruct(shape, bf16),
            jax.ShapeDtypeStruct(shape, bf16),
            jax.ShapeDtypeStruct(shape, bf16),
            jax.ShapeDtypeStruct((1, HEADS), f32),
        ],
        in_specs=[whole, whole] + [anywhere] * 5,
        out_specs=[anywhere] * 3 + [whole],
        scratch_shapes=[
            pltpu.VMEM((2, TOK, DH), bf16),
            pltpu.VMEM((2, TOK, DH), bf16),
            pltpu.VMEM((2, TOK, DH), bf16),
            pltpu.VMEM((2, NDEV, 2, HALF, DH), bf16),
            pltpu.VMEM((NDEV, 1, ROWS), jnp.int32),
            pltpu.VMEM((TOK, DH), bf16),
            pltpu.VMEM((DH, TOK), bf16),
            pltpu.VMEM((TOK, BQ), f32),
            pltpu.VMEM((TOK, BQ), f32),
            pltpu.VMEM((TOK, BQ), bf16),
            pltpu.VMEM((TOK, DH), f32),
            pltpu.VMEM((TOK, DH), f32),
            pltpu.VMEM((2, TOK, DH), bf16),
            pltpu.VMEM((2, TOK, DH), bf16),
            pltpu.VMEM((2, TOK, DH), bf16),
            pltpu.VMEM((2, 1, DH), f32),
            pltpu.VMEM((HEADS, 1, DH), f32),
            pltpu.VMEM((1, DH), f32),
            pltpu.VMEM((1, DH), f32),
            dma((HEADS,)),
            dma((2, 4)),
            dma((2,)), dma((2,)),
            dma, dma,
            dma((2, 3)),
            dma((3,)),
            dma, dma,
            dma((2,)), dma,
        ],
        compiler_params=pltpu.CompilerParams(
            collective_id=0, has_side_effects=True, vmem_limit_bytes=60 * 1024 * 1024
        ),
        cost_estimate=pl.CostEstimate(
            flops=7_000_000_000, bytes_accessed=5_000_000, transcendentals=5_000_000
        ),
    )(
        router_logits.reshape(1, HEADS), gate_plan.reshape(1, HEADS),
        queries, keys, values, cotangent, merge_sizes.reshape(1, ROWS),
    )
    dq, dk, dv, r = pl.pallas_call(
        hand_over,
        out_shape=[jax.ShapeDtypeStruct(shape, bf16)] * 3
        + [jax.ShapeDtypeStruct((1, HEADS), f32)],
        in_specs=[anywhere] * 4,
        out_specs=[anywhere] * 4,
        scratch_shapes=[
            pltpu.VMEM((3,) + shape[1:], bf16), pltpu.VMEM((1, HEADS), f32), dma((7,)), dma((7,)),
        ],
        compiler_params=pltpu.CompilerParams(vmem_limit_bytes=60 * 1024 * 1024),
    )(dq, dk, dv, r)
    return (dq, dk, dv, r.reshape(HEADS))


def solution(mesh):
    return jax.shard_map(
        body,
        mesh=mesh,
        in_specs=(
            P("step", ("grp", "ctx"), None),
            P("step", ("grp", "ctx"), None),
            P("step", ("grp", "ctx"), None),
            P(("grp", "ctx"), None),
            P(("grp", "ctx")),
            P(),
            P(),
        ),
        out_specs=(
            P("step", ("grp", "ctx"), None),
            P("step", ("grp", "ctx"), None),
            P("step", ("grp", "ctx"), None),
            P("grp"),
        ),
        check_vma=False,
    )
```

```python
import functools
import math

import jax
import jax.numpy as jnp
from jax import lax
from jax.experimental import pallas as pl
from jax.experimental.pallas import tpu as pltpu
from jax.sharding import PartitionSpec as P

MESH = pl.DeviceIdType.MESH
DH = 128
NDEV = 16
ROWS = 128
TOK = NDEV * ROWS
HEADS = 20
BQ = 512
CK = 1024
HALF = ROWS // 2
UNITS = TOK // BQ
SCALE = DH ** -0.5
NT = (((1,), (1,)), ((), ()))


def owner_of(h, core):
    early = h < 8
    last = h >= 16
    i = jnp.where(early, h, h - 8)
    z = 2 * (i // 2) + jnp.where(early, core, 1 - core)
    x = i % 2
    j = h - 16
    z = jnp.where(last, 2 * j + core, z)
    x = jnp.where(last, core, x)
    return z * 2 + x


def kernel(
    logit_ref, gate_ref, q_ref, k_ref, v_ref, g_ref, ms_ref,
    dq_out, dk_out, dv_out, r_out,
    qb, kb, vb, gb, msb, kx, kt, s_buf, o_buf, ds_buf, dk_acc, dv_acc,
    dqs, dks, dvs, rmine, rb, rrow, rother,
    in_send, in_recv, q_recv, gf_send, gf_recv, ms_send, ms_recv, out_send, out_recv,
    rp_send, rp_recv, rb_send, rb_recv,
):
    me = lax.axis_index("ctx")
    step = lax.axis_index("step")
    core = lax.axis_index("grp") % 2
    z = me // 2
    x = me % 2
    early = (z + core) % 2 == 0
    double = jnp.logical_and(early, x == core)
    first_head = jnp.where(early, 0, 8) + (z // 2) * 2 + x
    second_head = 16 + z // 2
    n_slots = jnp.where(double, 2, 1)

    barrier = pltpu.get_barrier_semaphore()

    def greet(j, _):
        pl.semaphore_signal(
            barrier, inc=1, device_id={"ctx": (me + j) % NDEV}, device_id_type=MESH
        )
        return 0

    lax.fori_loop(1, NDEV, greet, 0)
    pl.semaphore_signal(barrier, inc=1, device_id={"step": 1 - step}, device_id_type=MESH)
    pl.semaphore_wait(barrier, NDEV)

    my_rows = pl.ds(pl.multiple_of(me * ROWS, ROWS), ROWS)

    def ms_copy(j):
        return pltpu.make_async_remote_copy(
            src_ref=ms_ref, dst_ref=msb.at[me], send_sem=ms_send, recv_sem=ms_recv,
            device_id={"ctx": (me + j) % NDEV}, device_id_type=MESH,
        )

    def send_ms(j, _):
        ms_copy(j).start()
        return 0

    lax.fori_loop(1, NDEV, send_ms, 0)
    pltpu.make_async_copy(ms_ref, msb.at[me], ms_recv).start()

    def send_pairs(h, pairs):
        owner = owner_of(h, core)

        @pl.when(owner == me)
        def _():
            for src, dst, sem in pairs:
                pltpu.make_async_copy(src, dst, sem).start()

        @pl.when(owner != me)
        def _():
            for src, dst, sem in pairs:
                pltpu.make_async_remote_copy(
                    src_ref=src, dst_ref=dst, send_sem=in_send.at[h], recv_sem=sem,
                    device_id={"ctx": owner}, device_id_type=MESH,
                ).start()

    def columns(h):
        return pl.ds(pl.multiple_of(h * DH, DH), DH)

    def send_g(h):
        slot = h // 16
        rows = pl.ds(pl.multiple_of(step * HALF, HALF), HALF)
        send_pairs(h, ((g_ref.at[rows, columns(h)], gb.at[slot, me, step], in_recv.at[slot, 3]),))

    def send_kv(h):
        slot = h // 16
        cols = columns(h)
        send_pairs(h, (
            (k_ref.at[0, :, cols], kb.at[slot, my_rows], in_recv.at[slot, 0]),
            (v_ref.at[0, :, cols], vb.at[slot, my_rows], in_recv.at[slot, 1]),
        ))

    def send_q(h):
        slot = h // 16
        send_pairs(h, ((q_ref.at[0, :, columns(h)], qb.at[slot, my_rows], q_recv.at[slot, me // 4]),))

    def loop(send, first, count, start):
        def one(j, _):
            send(first + (start + j) % count)
            return 0

        lax.fori_loop(0, count, one, 0)

    loop(send_g, 0, 8, z)
    loop(send_g, 16, 4, z // 2)
    loop(send_kv, 0, 8, z)
    loop(send_q, 0, 8, z)
    loop(send_g, 8, 8, z)
    loop(send_kv, 16, 4, z // 2)
    loop(send_q, 16, 4, z // 2)
    loop(send_kv, 8, 8, z)
    loop(send_q, 8, 8, z)

    def forward_g(slot):
        return pltpu.make_async_remote_copy(
            src_ref=gb.at[slot, :, step], dst_ref=gb.at[slot, :, step],
            send_sem=gf_send.at[slot], recv_sem=gf_recv.at[slot],
            device_id={"step": 1 - step}, device_id_type=MESH,
        )

    pltpu.make_async_copy(msb, msb, ms_recv).wait()
    lane = lax.broadcasted_iota(jnp.int32, (ROWS, ROWS), 1)
    row = lax.broadcasted_iota(jnp.int32, (ROWS, ROWS), 0)

    def extend(t, _):
        logs = jnp.log(msb[t].astype(jnp.float32)) * (1.0 / SCALE)
        spread = jnp.where(lane == row, jnp.broadcast_to(logs, (ROWS, ROWS)), 0.0)
        column = jnp.sum(spread, axis=1, keepdims=True)
        hi = column.astype(jnp.bfloat16).astype(jnp.float32)
        rest = column - hi
        mid = rest.astype(jnp.bfloat16).astype(jnp.float32)
        low = rest - mid
        ext = jnp.where(lane == 0, hi, jnp.where(lane == 1, mid, jnp.where(lane == 2, low, 0.0)))
        kx[pl.ds(pl.multiple_of(t * ROWS, ROWS), ROWS), :] = ext.astype(jnp.bfloat16)
        return 0

    lax.fori_loop(0, NDEV, extend, 0)

    def pass_g_on(slot, _):
        half = gb.at[slot, :, step]
        pltpu.make_async_copy(half, half, in_recv.at[slot, 3]).wait()
        forward_g(slot).start()
        return 0

    lax.fori_loop(0, n_slots, pass_g_on, 0)

    beta = jnp.where(gate_ref[...] == 1, jax.nn.sigmoid(logit_ref[...]), 1.0)
    coef_row = jnp.where(step == 1, beta, 1.0 - beta)
    head_lane = lax.broadcasted_iota(jnp.int32, (1, HEADS), 1)
    ones = jnp.ones((BQ, DH), jnp.bfloat16)

    def do_slot(slot, _):
        h = jnp.where(slot == 0, first_head, second_head)
        coef = jnp.sum(jnp.where(head_lane == h, coef_row, 0.0), axis=1, keepdims=True)
        cols = columns(h)
        for a, buf in enumerate((kb, vb)):
            pltpu.make_async_copy(buf.at[slot], buf.at[slot], in_recv.at[slot, a]).wait()
        forward_g(slot).wait_recv()

        def transpose_keys(t, _):
            rows = pl.ds(pl.multiple_of(t * ROWS, ROWS), ROWS)
            kt[:, rows] = kb[slot, rows, :].astype(jnp.float32).T.astype(jnp.bfloat16)
            dk_acc[rows, :] = jnp.zeros((ROWS, DH), jnp.float32)
            dv_acc[rows, :] = jnp.zeros((ROWS, DH), jnp.float32)
            return 0

        lax.fori_loop(0, NDEV, transpose_keys, 0)

        def send_rows(src_buf, dst_out, a, t):
            rows = pl.ds(pl.multiple_of(t * ROWS, ROWS), ROWS)
            src = src_buf.at[slot, rows]
            dst = dst_out.at[0, :, cols]

            @pl.when(t == me)
            def _():
                pltpu.make_async_copy(src, dst, out_recv.at[a]).start()

            @pl.when(t != me)
            def _():
                pltpu.make_async_remote_copy(
                    src_ref=src, dst_ref=dst, send_sem=out_send.at[slot, a],
                    recv_sem=out_recv.at[a], device_id={"ctx": t}, device_id_type=MESH,
                ).start()

        def unit(b, r_sum):
            q_rows = pl.ds(pl.multiple_of(b * BQ, BQ), BQ)
            q_in = qb.at[slot, q_rows]
            pltpu.make_async_copy(q_in, q_in, q_recv.at[slot, b]).wait()
            g_blk = gb[slot, pl.ds(b * (BQ // ROWS), BQ // ROWS)].reshape(BQ, DH)
            q_ext = jnp.concatenate([qb[slot, q_rows, :], ones], axis=1)

            def pass1(c, top):
                rows = pl.ds(pl.multiple_of(c * CK, CK), CK)
                k_ext = jnp.concatenate([kb[slot, rows, :], kx[rows, :]], axis=1)
                s = lax.dot_general(k_ext, q_ext, NT, preferred_element_type=jnp.float32)
                s_buf[rows, :] = s
                return jnp.maximum(top, jnp.max(s.reshape(CK // 8, 8, BQ), axis=0))

            top = lax.fori_loop(
                0, TOK // CK, pass1, jnp.full((8, BQ), -jnp.inf, jnp.float32)
            )
            top = jnp.max(top, axis=0, keepdims=True)

            def pass2(c, carry):
                l_sum, rd_sum = carry
                rows = pl.ds(pl.multiple_of(c * CK, CK), CK)
                o = lax.dot_general(
                    vb[slot, rows, :], g_blk, NT,
                    preferred_element_type=jnp.float32,
                )
                e = jnp.exp2((s_buf[rows, :] - top) * (SCALE * math.log2(math.e)))
                s_buf[rows, :] = e
                o_buf[rows, :] = o
                l_sum = l_sum + jnp.sum(e.reshape(CK // 8, 8, BQ), axis=0)
                rd_sum = rd_sum + jnp.sum((e * o).reshape(CK // 8, 8, BQ), axis=0)
                return (l_sum, rd_sum)

            zero = jnp.zeros((8, BQ), jnp.float32)
            l_sum, rd_sum = lax.fori_loop(0, TOK // CK, pass2, (zero, zero))
            inv = 1.0 / jnp.sum(l_sum, axis=0, keepdims=True)
            rd = jnp.sum(rd_sum, axis=0, keepdims=True) * inv
            for i in range(BQ // DH):
                r_sum = r_sum + rd[:, i * DH:(i + 1) * DH]

            @pl.when(b == UNITS - 1)
            def _():
                rmine[slot] = r_sum

                def send_r(j, _):
                    pltpu.make_async_remote_copy(
                        src_ref=rmine.at[slot], dst_ref=rb.at[h],
                        send_sem=rb_send.at[slot], recv_sem=rb_recv,
                        device_id={"ctx": (me + j) % NDEV}, device_id_type=MESH,
                    ).start()
                    return 0

                lax.fori_loop(1, NDEV, send_r, 0)
                pltpu.make_async_copy(rmine.at[slot], rb.at[h], rb_recv).start()

            inv = inv * coef
            inv_col = jnp.concatenate(
                [
                    jnp.broadcast_to(inv[:, i * DH:(i + 1) * DH], (DH, DH)).T
                    for i in range(BQ // DH)
                ],
                axis=0,
            )
            g_scaled = (g_blk.astype(jnp.float32) * inv_col).astype(jnp.bfloat16)
            inv_col = inv_col * SCALE
            q_scaled = (qb[slot, q_rows, :].astype(jnp.float32) * inv_col).astype(jnp.bfloat16)

            def pass3(c, _):
                rows = pl.ds(pl.multiple_of(c * CK, CK), CK)
                e = s_buf[rows, :]
                ds = (e * (o_buf[rows, :] - rd)).astype(jnp.bfloat16)
                ds_buf[rows, :] = ds
                dv_acc[rows, :] += jnp.dot(
                    e.astype(jnp.bfloat16), g_scaled, preferred_element_type=jnp.float32
                )
                dk_acc[rows, :] += jnp.dot(ds, q_scaled, preferred_element_type=jnp.float32)
                return 0

            def finish(t, _):
                t = (t // 4) * 4 + (t + me) % 4
                rows = pl.ds(pl.multiple_of(t * ROWS, ROWS), ROWS)
                dks[slot, rows, :] = dk_acc[rows, :].astype(jnp.bfloat16)
                dvs[slot, rows, :] = dv_acc[rows, :].astype(jnp.bfloat16)
                send_rows(dks, dk_out, 1, t)
                send_rows(dvs, dv_out, 2, t)
                return 0

            def pass3_send(c, _):
                pass3(c, 0)

                @pl.when(b == UNITS - 1)
                def _():
                    lax.fori_loop(c * (CK // ROWS), (c + 1) * (CK // ROWS), finish, 0)

                return 0

            lax.fori_loop(0, TOK // CK, pass3_send, 0)
            dqt = jnp.dot(kt[...], ds_buf[...], preferred_element_type=jnp.float32)
            dqs[slot, q_rows, :] = (dqt.T * inv_col).astype(jnp.bfloat16)

            def send_dq(i, _):
                send_rows(dqs, dq_out, 0, b * (BQ // ROWS) + i)
                return 0

            lax.fori_loop(0, BQ // ROWS, send_dq, 0)
            return r_sum

        lax.fori_loop(0, UNITS, unit, jnp.zeros((1, DH), jnp.float32))
        return 0

    lax.fori_loop(0, n_slots, do_slot, 0)

    pltpu.make_async_copy(rb, rb, rb_recv).wait()
    sums = jnp.sum(rb[...], axis=2)
    diagonal = (
        lax.broadcasted_iota(jnp.int32, (HEADS, DH), 0)
        == lax.broadcasted_iota(jnp.int32, (HEADS, DH), 1)
    )
    rrow[...] = jnp.sum(jnp.where(diagonal, sums, 0.0), axis=0, keepdims=True)
    to_partner = pltpu.make_async_remote_copy(
        src_ref=rrow, dst_ref=rother, send_sem=rp_send, recv_sem=rp_recv,
        device_id={"step": 1 - step}, device_id_type=MESH,
    )
    to_partner.start()

    pltpu.make_async_copy(msb.at[pl.ds(0, NDEV - 1)], msb.at[pl.ds(0, NDEV - 1)], ms_send).wait()

    sent = kb.at[0, pl.ds(0, 3 * ROWS + HALF)]

    def sent_head(h, _):
        @pl.when(owner_of(h, core) != me)
        def _():
            pltpu.make_async_copy(
                sent, sent, in_send.at[h]
            ).wait()

        return 0

    lax.fori_loop(0, HEADS, sent_head, 0)

    def sent_slot(slot, _):
        for a, buf in enumerate((dqs, dks, dvs)):
            part = buf.at[slot, pl.ds(0, TOK - ROWS)]
            pltpu.make_async_copy(part, part, out_send.at[slot, a]).wait()
        part = rb.at[pl.ds(0, NDEV - 1)]
        pltpu.make_async_copy(part, part, rb_send.at[slot]).wait()
        forward_g(slot).wait_send()
        return 0

    lax.fori_loop(0, n_slots, sent_slot, 0)

    to_partner.wait()
    sign = jnp.where(step == 1, 1.0, -1.0).astype(jnp.float32)
    total = (rrow[...] - rother[...]) * sign
    r_out[...] = beta * (1.0 - beta) * total[:, :HEADS] * (1.0 / math.sqrt(TOK))
    for a, out in enumerate((dq_out, dk_out, dv_out)):
        pltpu.make_async_copy(out, out, out_recv.at[a]).wait()


def body(queries, keys, values, cotangent, merge_sizes, router_logits, gate_plan):
    shape = queries.shape
    bf16, f32 = jnp.bfloat16, jnp.float32
    anywhere = pl.BlockSpec(memory_space=pl.ANY)
    whole = pl.BlockSpec(memory_space=pltpu.VMEM)
    dma = pltpu.SemaphoreType.DMA
    dq, dk, dv, r = pl.pallas_call(
        kernel,
        out_shape=[
            pltpu.VMEM(shape, bf16),
            pltpu.VMEM(shape, bf16),
            pltpu.VMEM(shape, bf16),
            pltpu.VMEM((1, HEADS), f32),
        ],
        in_specs=[whole, whole] + [anywhere] * 5,
        out_specs=[whole] * 4,
        scratch_shapes=[
            pltpu.VMEM((2, TOK, DH), bf16),
            pltpu.VMEM((2, TOK, DH), bf16),
            pltpu.VMEM((2, TOK, DH), bf16),
            pltpu.VMEM((2, NDEV, 2, HALF, DH), bf16),
            pltpu.VMEM((NDEV, 1, ROWS), jnp.int32),
            pltpu.VMEM((TOK, DH), bf16),
            pltpu.VMEM((DH, TOK), bf16),
            pltpu.VMEM((TOK, BQ), f32),
            pltpu.VMEM((TOK, BQ), f32),
            pltpu.VMEM((TOK, BQ), bf16),
            pltpu.VMEM((TOK, DH), f32),
            pltpu.VMEM((TOK, DH), f32),
            pltpu.VMEM((2, TOK, DH), bf16),
            pltpu.VMEM((2, TOK, DH), bf16),
            pltpu.VMEM((2, TOK, DH), bf16),
            pltpu.VMEM((2, 1, DH), f32),
            pltpu.VMEM((HEADS, 1, DH), f32),
            pltpu.VMEM((1, DH), f32),
            pltpu.VMEM((1, DH), f32),
            dma((HEADS,)),
            dma((2, 4)),
            dma((2, UNITS)),
            dma((2,)), dma((2,)),
            dma, dma,
            dma((2, 3)),
            dma((3,)),
            dma, dma,
            dma((2,)), dma,
        ],
        compiler_params=pltpu.CompilerParams(
            collective_id=0, has_side_effects=True, vmem_limit_bytes=60 * 1024 * 1024
        ),
        cost_estimate=pl.CostEstimate(
            flops=7_000_000_000, bytes_accessed=5_000_000, transcendentals=5_000_000
        ),
    )(
        router_logits.reshape(1, HEADS), gate_plan.reshape(1, HEADS),
        queries, keys, values, cotangent, merge_sizes.reshape(1, ROWS),
    )
    return (dq, dk, dv, r.reshape(HEADS))


def solution(mesh):
    return jax.shard_map(
        body,
        mesh=mesh,
        in_specs=(
            P("step", ("grp", "ctx"), None),
            P("step", ("grp", "ctx"), None),
            P("step", ("grp", "ctx"), None),
            P(("grp", "ctx"), None),
            P(("grp", "ctx")),
            P(),
            P(),
        ),
        out_specs=(
            P("step", ("grp", "ctx"), None),
            P("step", ("grp", "ctx"), None),
            P("step", ("grp", "ctx"), None),
            P("grp"),
        ),
        check_vma=False,
    )
```

```python
import functools
import math

import jax
import jax.numpy as jnp
from jax import lax
from jax.experimental import pallas as pl
from jax.experimental.pallas import tpu as pltpu
from jax.sharding import PartitionSpec as P

MESH = pl.DeviceIdType.MESH
DH = 128
NDEV = 16
ROWS = 128
TOK = NDEV * ROWS
HEADS = 20
BQ = 512
CK = 1024
HALF = ROWS // 2
UNITS = TOK // BQ
SCALE = DH ** -0.5
NT = (((1,), (1,)), ((), ()))


def owner_of(h, core):
    early = h < 8
    last = h >= 16
    i = jnp.where(early, h, h - 8)
    z = 2 * (i // 2) + jnp.where(early, core, 1 - core)
    x = i % 2
    j = h - 16
    z = jnp.where(last, 2 * j + core, z)
    x = jnp.where(last, core, x)
    return z * 2 + x


def kernel(
    logit_in, gate_in, q_ref, k_ref, v_ref, g_ref, ms_ref,
    dq_out, dk_out, dv_out, r_out,
    qb, kb, vb, gb, msb, kx, kt, s_buf, o_buf, ds_buf, dk_acc, dv_acc,
    dqs, dks, dvs, rmine, rb, rrow, rother, logit_ref, gate_ref,
    in_send, in_recv, q_recv, gf_send, gf_recv, ms_send, ms_recv, out_send, out_recv,
    rp_send, rp_recv, rb_send, rb_recv, small_sem,
):
    me = lax.axis_index("ctx")
    step = lax.axis_index("step")
    core = lax.axis_index("grp") % 2
    z = me // 2
    x = me % 2
    early = (z + core) % 2 == 0
    double = jnp.logical_and(early, x == core)
    first_head = jnp.where(early, 0, 8) + (z // 2) * 2 + x
    second_head = 16 + z // 2
    n_slots = jnp.where(double, 2, 1)

    barrier = pltpu.get_barrier_semaphore()

    def greet(j, _):
        pl.semaphore_signal(
            barrier, inc=1, device_id={"ctx": (me + j) % NDEV}, device_id_type=MESH
        )
        return 0

    lax.fori_loop(1, NDEV, greet, 0)
    pl.semaphore_signal(barrier, inc=1, device_id={"step": 1 - step}, device_id_type=MESH)
    small = (
        pltpu.make_async_copy(logit_in, logit_ref, small_sem.at[0]),
        pltpu.make_async_copy(gate_in, gate_ref, small_sem.at[1]),
    )
    for copy in small:
        copy.start()
    pl.semaphore_wait(barrier, NDEV)

    my_rows = pl.ds(pl.multiple_of(me * ROWS, ROWS), ROWS)

    def ms_copy(j):
        return pltpu.make_async_remote_copy(
            src_ref=ms_ref, dst_ref=msb.at[me], send_sem=ms_send, recv_sem=ms_recv,
            device_id={"ctx": (me + j) % NDEV}, device_id_type=MESH,
        )

    def send_ms(j, _):
        ms_copy(j).start()
        return 0

    lax.fori_loop(1, NDEV, send_ms, 0)
    pltpu.make_async_copy(ms_ref, msb.at[me], ms_recv).start()

    def send_pairs(h, pairs):
        owner = owner_of(h, core)

        @pl.when(owner == me)
        def _():
            for src, dst, sem in pairs:
                pltpu.make_async_copy(src, dst, sem).start()

        @pl.when(owner != me)
        def _():
            for src, dst, sem in pairs:
                pltpu.make_async_remote_copy(
                    src_ref=src, dst_ref=dst, send_sem=in_send.at[h], recv_sem=sem,
                    device_id={"ctx": owner}, device_id_type=MESH,
                ).start()

    def columns(h):
        return pl.ds(pl.multiple_of(h * DH, DH), DH)

    def send_g(h):
        slot = h // 16
        rows = pl.ds(pl.multiple_of(step * HALF, HALF), HALF)
        send_pairs(h, ((g_ref.at[rows, columns(h)], gb.at[slot, me, step], in_recv.at[slot, 3]),))

    def send_kv(h):
        slot = h // 16
        cols = columns(h)
        send_pairs(h, (
            (k_ref.at[0, :, cols], kb.at[slot, my_rows], in_recv.at[slot, 0]),
            (v_ref.at[0, :, cols], vb.at[slot, my_rows], in_recv.at[slot, 1]),
        ))

    def send_q(h):
        slot = h // 16
        send_pairs(h, ((q_ref.at[0, :, columns(h)], qb.at[slot, my_rows], q_recv.at[slot, me // 4]),))

    def loop(send, first, count, start):
        def one(j, _):
            send(first + (start + j) % count)
            return 0

        lax.fori_loop(0, count, one, 0)

    loop(send_g, 0, 8, z)
    loop(send_g, 16, 4, z // 2)
    loop(send_kv, 0, 8, z)
    loop(send_q, 0, 8, z)
    loop(send_g, 8, 8, z)
    loop(send_kv, 16, 4, z // 2)
    loop(send_q, 16, 4, z // 2)
    loop(send_kv, 8, 8, z)
    loop(send_q, 8, 8, z)

    def forward_g(slot):
        return pltpu.make_async_remote_copy(
            src_ref=gb.at[slot, :, step], dst_ref=gb.at[slot, :, step],
            send_sem=gf_send.at[slot], recv_sem=gf_recv.at[slot],
            device_id={"step": 1 - step}, device_id_type=MESH,
        )

    pltpu.make_async_copy(msb, msb, ms_recv).wait()
    lane = lax.broadcasted_iota(jnp.int32, (ROWS, ROWS), 1)
    row = lax.broadcasted_iota(jnp.int32, (ROWS, ROWS), 0)

    def extend(t, _):
        logs = jnp.log(msb[t].astype(jnp.float32)) * (1.0 / SCALE)
        spread = jnp.where(lane == row, jnp.broadcast_to(logs, (ROWS, ROWS)), 0.0)
        column = jnp.sum(spread, axis=1, keepdims=True)
        hi = column.astype(jnp.bfloat16).astype(jnp.float32)
        rest = column - hi
        mid = rest.astype(jnp.bfloat16).astype(jnp.float32)
        low = rest - mid
        ext = jnp.where(lane == 0, hi, jnp.where(lane == 1, mid, jnp.where(lane == 2, low, 0.0)))
        kx[pl.ds(pl.multiple_of(t * ROWS, ROWS), ROWS), :] = ext.astype(jnp.bfloat16)
        return 0

    lax.fori_loop(0, NDEV, extend, 0)

    def pass_g_on(slot, _):
        half = gb.at[slot, :, step]
        pltpu.make_async_copy(half, half, in_recv.at[slot, 3]).wait()
        forward_g(slot).start()
        return 0

    lax.fori_loop(0, n_slots, pass_g_on, 0)

    for copy in small:
        copy.wait()
    beta = jnp.where(gate_ref[...] == 1, jax.nn.sigmoid(logit_ref[...]), 1.0)
    coef_row = jnp.where(step == 1, beta, 1.0 - beta)
    head_lane = lax.broadcasted_iota(jnp.int32, (1, HEADS), 1)
    ones = jnp.ones((BQ, DH), jnp.bfloat16)

    def do_slot(slot, _):
        h = jnp.where(slot == 0, first_head, second_head)
        coef = jnp.sum(jnp.where(head_lane == h, coef_row, 0.0), axis=1, keepdims=True)
        cols = columns(h)
        for a, buf in enumerate((kb, vb)):
            pltpu.make_async_copy(buf.at[slot], buf.at[slot], in_recv.at[slot, a]).wait()
        forward_g(slot).wait_recv()

        def transpose_keys(t, _):
            rows = pl.ds(pl.multiple_of(t * ROWS, ROWS), ROWS)
            kt[:, rows] = kb[slot, rows, :].astype(jnp.float32).T.astype(jnp.bfloat16)
            dk_acc[rows, :] = jnp.zeros((ROWS, DH), jnp.float32)
            dv_acc[rows, :] = jnp.zeros((ROWS, DH), jnp.float32)
            return 0

        lax.fori_loop(0, NDEV, transpose_keys, 0)

        def send_rows(src_buf, dst_out, a, t):
            rows = pl.ds(pl.multiple_of(t * ROWS, ROWS), ROWS)
            src = src_buf.at[slot, rows]
            dst = dst_out.at[0, :, cols]

            @pl.when(t == me)
            def _():
                pltpu.make_async_copy(src, dst, out_recv.at[a]).start()

            @pl.when(t != me)
            def _():
                pltpu.make_async_remote_copy(
                    src_ref=src, dst_ref=dst, send_sem=out_send.at[slot, a],
                    recv_sem=out_recv.at[a], device_id={"ctx": t}, device_id_type=MESH,
                ).start()

        def unit(b, r_sum):
            q_rows = pl.ds(pl.multiple_of(b * BQ, BQ), BQ)
            q_in = qb.at[slot, q_rows]
            pltpu.make_async_copy(q_in, q_in, q_recv.at[slot, b]).wait()
            g_blk = gb[slot, pl.ds(b * (BQ // ROWS), BQ // ROWS)].reshape(BQ, DH)
            q_ext = jnp.concatenate([qb[slot, q_rows, :], ones], axis=1)

            def pass1(c, top):
                rows = pl.ds(pl.multiple_of(c * CK, CK), CK)
                k_ext = jnp.concatenate([kb[slot, rows, :], kx[rows, :]], axis=1)
                s = lax.dot_general(k_ext, q_ext, NT, preferred_element_type=jnp.float32)
                s_buf[rows, :] = s
                return jnp.maximum(top, jnp.max(s.reshape(CK // 8, 8, BQ), axis=0))

            top = lax.fori_loop(
                0, TOK // CK, pass1, jnp.full((8, BQ), -jnp.inf, jnp.float32)
            )
            top = jnp.max(top, axis=0, keepdims=True)

            def pass2(c, carry):
                l_sum, rd_sum = carry
                rows = pl.ds(pl.multiple_of(c * CK, CK), CK)
                o = lax.dot_general(
                    vb[slot, rows, :], g_blk, NT,
                    preferred_element_type=jnp.float32,
                )
                e = jnp.exp2((s_buf[rows, :] - top) * (SCALE * math.log2(math.e)))
                s_buf[rows, :] = e
                o_buf[rows, :] = o
                l_sum = l_sum + jnp.sum(e.reshape(CK // 8, 8, BQ), axis=0)
                rd_sum = rd_sum + jnp.sum((e * o).reshape(CK // 8, 8, BQ), axis=0)
                return (l_sum, rd_sum)

            zero = jnp.zeros((8, BQ), jnp.float32)
            l_sum, rd_sum = lax.fori_loop(0, TOK // CK, pass2, (zero, zero))
            inv = 1.0 / jnp.sum(l_sum, axis=0, keepdims=True)
            rd = jnp.sum(rd_sum, axis=0, keepdims=True) * inv
            for i in range(BQ // DH):
                r_sum = r_sum + rd[:, i * DH:(i + 1) * DH]

            @pl.when(b == UNITS - 1)
            def _():
                rmine[slot] = r_sum

                def send_r(j, _):
                    pltpu.make_async_remote_copy(
                        src_ref=rmine.at[slot], dst_ref=rb.at[h],
                        send_sem=rb_send.at[slot], recv_sem=rb_recv,
                        device_id={"ctx": (me + j) % NDEV}, device_id_type=MESH,
                    ).start()
                    return 0

                lax.fori_loop(1, NDEV, send_r, 0)
                pltpu.make_async_copy(rmine.at[slot], rb.at[h], rb_recv).start()

            inv = inv * coef
            inv_col = jnp.concatenate(
                [
                    jnp.broadcast_to(inv[:, i * DH:(i + 1) * DH], (DH, DH)).T
                    for i in range(BQ // DH)
                ],
                axis=0,
            )
            g_scaled = (g_blk.astype(jnp.float32) * inv_col).astype(jnp.bfloat16)
            inv_col = inv_col * SCALE
            q_scaled = (qb[slot, q_rows, :].astype(jnp.float32) * inv_col).astype(jnp.bfloat16)

            def pass3(c, _):
                rows = pl.ds(pl.multiple_of(c * CK, CK), CK)
                e = s_buf[rows, :]
                ds = (e * (o_buf[rows, :] - rd)).astype(jnp.bfloat16)
                ds_buf[rows, :] = ds
                dv_acc[rows, :] += jnp.dot(
                    e.astype(jnp.bfloat16), g_scaled, preferred_element_type=jnp.float32
                )
                dk_acc[rows, :] += jnp.dot(ds, q_scaled, preferred_element_type=jnp.float32)
                return 0

            def finish(t, _):
                t = (t // 4) * 4 + (t + me) % 4
                rows = pl.ds(pl.multiple_of(t * ROWS, ROWS), ROWS)
                dks[slot, rows, :] = dk_acc[rows, :].astype(jnp.bfloat16)
                dvs[slot, rows, :] = dv_acc[rows, :].astype(jnp.bfloat16)
                send_rows(dks, dk_out, 1, t)
                send_rows(dvs, dv_out, 2, t)
                return 0

            def pass3_send(c, _):
                pass3(c, 0)

                @pl.when(b == UNITS - 1)
                def _():
                    lax.fori_loop(c * (CK // ROWS), (c + 1) * (CK // ROWS), finish, 0)

                return 0

            lax.fori_loop(0, TOK // CK, pass3_send, 0)
            dqt = jnp.dot(kt[...], ds_buf[...], preferred_element_type=jnp.float32)
            dqs[slot, q_rows, :] = (dqt.T * inv_col).astype(jnp.bfloat16)

            def send_dq(i, _):
                send_rows(dqs, dq_out, 0, b * (BQ // ROWS) + i)
                return 0

            lax.fori_loop(0, BQ // ROWS, send_dq, 0)
            return r_sum

        lax.fori_loop(0, UNITS, unit, jnp.zeros((1, DH), jnp.float32))
        return 0

    lax.fori_loop(0, n_slots, do_slot, 0)

    pltpu.make_async_copy(rb, rb, rb_recv).wait()
    sums = jnp.sum(rb[...], axis=2)
    diagonal = (
        lax.broadcasted_iota(jnp.int32, (HEADS, DH), 0)
        == lax.broadcasted_iota(jnp.int32, (HEADS, DH), 1)
    )
    rrow[...] = jnp.sum(jnp.where(diagonal, sums, 0.0), axis=0, keepdims=True)
    to_partner = pltpu.make_async_remote_copy(
        src_ref=rrow, dst_ref=rother, send_sem=rp_send, recv_sem=rp_recv,
        device_id={"step": 1 - step}, device_id_type=MESH,
    )
    to_partner.start()

    pltpu.make_async_copy(msb.at[pl.ds(0, NDEV - 1)], msb.at[pl.ds(0, NDEV - 1)], ms_send).wait()

    sent = kb.at[0, pl.ds(0, 3 * ROWS + HALF)]

    def sent_head(h, _):
        @pl.when(owner_of(h, core) != me)
        def _():
            pltpu.make_async_copy(
                sent, sent, in_send.at[h]
            ).wait()

        return 0

    lax.fori_loop(0, HEADS, sent_head, 0)

    def sent_slot(slot, _):
        for a, buf in enumerate((dqs, dks, dvs)):
            part = buf.at[slot, pl.ds(0, TOK - ROWS)]
            pltpu.make_async_copy(part, part, out_send.at[slot, a]).wait()
        part = rb.at[pl.ds(0, NDEV - 1)]
        pltpu.make_async_copy(part, part, rb_send.at[slot]).wait()
        forward_g(slot).wait_send()
        return 0

    lax.fori_loop(0, n_slots, sent_slot, 0)

    to_partner.wait()
    sign = jnp.where(step == 1, 1.0, -1.0).astype(jnp.float32)
    total = (rrow[...] - rother[...]) * sign
    r_out[...] = beta * (1.0 - beta) * total[:, :HEADS] * (1.0 / math.sqrt(TOK))
    for a, out in enumerate((dq_out, dk_out, dv_out)):
        pltpu.make_async_copy(out, out, out_recv.at[a]).wait()


def hand_over(dq_in, dk_in, dv_in, r_in, dq_out, dk_out, dv_out, r_out, sems):
    copies = [pltpu.make_async_copy(r_in, r_out, sems.at[0])]
    for a, (src, dst) in enumerate(((dq_in, dq_out), (dk_in, dk_out), (dv_in, dv_out))):
        for i in range(2):
            rows = pl.ds(i * HALF, HALF)
            copies.append(
                pltpu.make_async_copy(src.at[0, rows], dst.at[0, rows], sems.at[1 + 2 * a + i])
            )
    for copy in copies:
        copy.start()
    for copy in copies:
        copy.wait()


def body(queries, keys, values, cotangent, merge_sizes, router_logits, gate_plan):
    shape = queries.shape
    bf16, f32 = jnp.bfloat16, jnp.float32
    anywhere = pl.BlockSpec(memory_space=pl.ANY)
    whole = pl.BlockSpec(memory_space=pltpu.VMEM)
    dma = pltpu.SemaphoreType.DMA
    dq, dk, dv, r = pl.pallas_call(
        kernel,
        out_shape=[
            pltpu.VMEM(shape, bf16),
            pltpu.VMEM(shape, bf16),
            pltpu.VMEM(shape, bf16),
            pltpu.VMEM((1, HEADS), f32),
        ],
        in_specs=[anywhere] * 7,
        out_specs=[whole] * 4,
        scratch_shapes=[
            pltpu.VMEM((2, TOK, DH), bf16),
            pltpu.VMEM((2, TOK, DH), bf16),
            pltpu.VMEM((2, TOK, DH), bf16),
            pltpu.VMEM((2, NDEV, 2, HALF, DH), bf16),
            pltpu.VMEM((NDEV, 1, ROWS), jnp.int32),
            pltpu.VMEM((TOK, DH), bf16),
            pltpu.VMEM((DH, TOK), bf16),
            pltpu.VMEM((TOK, BQ), f32),
            pltpu.VMEM((TOK, BQ), f32),
            pltpu.VMEM((TOK, BQ), bf16),
            pltpu.VMEM((TOK, DH), f32),
            pltpu.VMEM((TOK, DH), f32),
            pltpu.VMEM((2, TOK, DH), bf16),
            pltpu.VMEM((2, TOK, DH), bf16),
            pltpu.VMEM((2, TOK, DH), bf16),
            pltpu.VMEM((2, 1, DH), f32),
            pltpu.VMEM((HEADS, 1, DH), f32),
            pltpu.VMEM((1, DH), f32),
            pltpu.VMEM((1, DH), f32),
            pltpu.VMEM((1, HEADS), f32),
            pltpu.VMEM((1, HEADS), jnp.int32),
            dma((HEADS,)),
            dma((2, 4)),
            dma((2, UNITS)),
            dma((2,)), dma((2,)),
            dma, dma,
            dma((2, 3)),
            dma((3,)),
            dma, dma,
            dma((2,)), dma,
            dma((2,)),
        ],
        compiler_params=pltpu.CompilerParams(
            collective_id=0, has_side_effects=True, vmem_limit_bytes=60 * 1024 * 1024
        ),
        cost_estimate=pl.CostEstimate(
            flops=7_000_000_000, bytes_accessed=5_000_000, transcendentals=5_000_000
        ),
    )(
        router_logits.reshape(1, HEADS), gate_plan.reshape(1, HEADS),
        queries, keys, values, cotangent, merge_sizes.reshape(1, ROWS),
    )
    held = [pltpu.with_memory_space_constraint(a, pltpu.VMEM) for a in (dq, dk, dv, r)]
    dq, dk, dv, r = pl.pallas_call(
        hand_over,
        out_shape=[jax.ShapeDtypeStruct(shape, bf16)] * 3
        + [jax.ShapeDtypeStruct((1, HEADS), f32)],
        in_specs=[whole] * 4,
        out_specs=[anywhere] * 4,
        scratch_shapes=[dma((7,))],
        compiler_params=pltpu.CompilerParams(vmem_limit_bytes=60 * 1024 * 1024),
    )(*held)
    return (dq, dk, dv, r.reshape(HEADS))


def solution(mesh):
    return jax.shard_map(
        body,
        mesh=mesh,
        in_specs=(
            P("step", ("grp", "ctx"), None),
            P("step", ("grp", "ctx"), None),
            P("step", ("grp", "ctx"), None),
            P(("grp", "ctx"), None),
            P(("grp", "ctx")),
            P(),
            P(),
        ),
        out_specs=(
            P("step", ("grp", "ctx"), None),
            P("step", ("grp", "ctx"), None),
            P("step", ("grp", "ctx"), None),
            P("grp"),
        ),
        check_vma=False,
    )
```

```python
import functools
import math

import jax
import jax.numpy as jnp
from jax import lax
from jax.experimental import pallas as pl
from jax.experimental.pallas import tpu as pltpu
from jax.sharding import PartitionSpec as P

MESH = pl.DeviceIdType.MESH
DH = 128
NDEV = 16
ROWS = 128
TOK = NDEV * ROWS
HEADS = 20
BQ = 512
CK = 1024
HALF = ROWS // 2
UNITS = TOK // BQ
SCALE = DH ** -0.5
NT = (((1,), (1,)), ((), ()))


def owner_of(h, core):
    early = h < 8
    last = h >= 16
    i = jnp.where(early, h, h - 8)
    z = 2 * (i // 2) + jnp.where(early, core, 1 - core)
    x = i % 2
    j = h - 16
    z = jnp.where(last, 2 * j + core, z)
    x = jnp.where(last, core, x)
    return z * 2 + x


def kernel(
    logit_in, gate_in, q_ref, k_ref, v_ref, g_ref, ms_ref,
    dq_out, dk_out, dv_out, r_out,
    qb, kb, vb, gb, msb, kx, kt, s_buf, o_buf, ds_buf, dk_acc, dv_acc,
    dqs, dks, dvs, rmine, rb, rrow, rother, logit_ref, gate_ref,
    in_send, in_recv, q_recv, gf_send, gf_recv, ms_send, ms_recv, out_send, out_recv,
    rp_send, rp_recv, rb_send, rb_recv, small_sem,
):
    me = lax.axis_index("ctx")
    step = lax.axis_index("step")
    core = lax.axis_index("grp") % 2
    z = me // 2
    x = me % 2
    early = (z + core) % 2 == 0
    double = jnp.logical_and(early, x == core)
    first_head = jnp.where(early, 0, 8) + (z // 2) * 2 + x
    second_head = 16 + z // 2
    n_slots = jnp.where(double, 2, 1)

    barrier = pltpu.get_barrier_semaphore()

    def greet(j, _):
        pl.semaphore_signal(
            barrier, inc=1, device_id={"ctx": (me + j) % NDEV}, device_id_type=MESH
        )
        return 0

    lax.fori_loop(1, NDEV, greet, 0)
    pl.semaphore_signal(barrier, inc=1, device_id={"step": 1 - step}, device_id_type=MESH)
    small = (
        pltpu.make_async_copy(logit_in, logit_ref, small_sem.at[0]),
        pltpu.make_async_copy(gate_in, gate_ref, small_sem.at[1]),
    )
    for copy in small:
        copy.start()
    pl.semaphore_wait(barrier, NDEV)

    my_rows = pl.ds(pl.multiple_of(me * ROWS, ROWS), ROWS)

    def ms_copy(j):
        return pltpu.make_async_remote_copy(
            src_ref=ms_ref, dst_ref=msb.at[me], send_sem=ms_send, recv_sem=ms_recv,
            device_id={"ctx": (me + j) % NDEV}, device_id_type=MESH,
        )

    def send_ms(j, _):
        ms_copy(j).start()
        return 0

    lax.fori_loop(1, NDEV, send_ms, 0)
    pltpu.make_async_copy(ms_ref, msb.at[me], ms_recv).start()

    def send_pairs(h, pairs):
        owner = owner_of(h, core)

        @pl.when(owner == me)
        def _():
            for src, dst, sem in pairs:
                pltpu.make_async_copy(src, dst, sem).start()

        @pl.when(owner != me)
        def _():
            for src, dst, sem in pairs:
                pltpu.make_async_remote_copy(
                    src_ref=src, dst_ref=dst, send_sem=in_send.at[h], recv_sem=sem,
                    device_id={"ctx": owner}, device_id_type=MESH,
                ).start()

    def columns(h):
        return pl.ds(pl.multiple_of(h * DH, DH), DH)

    def send_g(h):
        slot = h // 16
        rows = pl.ds(pl.multiple_of(step * HALF, HALF), HALF)
        send_pairs(h, ((g_ref.at[rows, columns(h)], gb.at[slot, me, step], in_recv.at[slot, 3]),))

    def send_kv(h):
        slot = h // 16
        cols = columns(h)
        send_pairs(h, (
            (k_ref.at[0, :, cols], kb.at[slot, my_rows], in_recv.at[slot, 0]),
            (v_ref.at[0, :, cols], vb.at[slot, my_rows], in_recv.at[slot, 1]),
        ))

    def send_q(h):
        slot = h // 16
        send_pairs(h, ((q_ref.at[0, :, columns(h)], qb.at[slot, my_rows], q_recv.at[slot, me // 4]),))

    def loop(send, first, count, start):
        def one(j, _):
            send(first + (start + j) % count)
            return 0

        lax.fori_loop(0, count, one, 0)

    loop(send_g, 0, 8, z)
    loop(send_g, 16, 4, z // 2)
    loop(send_kv, 0, 8, z)
    loop(send_q, 0, 8, z)
    loop(send_g, 8, 8, z)
    loop(send_kv, 16, 4, z // 2)
    loop(send_q, 16, 4, z // 2)
    loop(send_kv, 8, 8, z)
    loop(send_q, 8, 8, z)

    def forward_g(slot):
        return pltpu.make_async_remote_copy(
            src_ref=gb.at[slot, :, step], dst_ref=gb.at[slot, :, step],
            send_sem=gf_send.at[slot], recv_sem=gf_recv.at[slot],
            device_id={"step": 1 - step}, device_id_type=MESH,
        )

    pltpu.make_async_copy(msb, msb, ms_recv).wait()
    lane = lax.broadcasted_iota(jnp.int32, (ROWS, ROWS), 1)
    row = lax.broadcasted_iota(jnp.int32, (ROWS, ROWS), 0)

    def extend(t, _):
        logs = jnp.log(msb[t].astype(jnp.float32)) * (1.0 / SCALE)
        spread = jnp.where(lane == row, jnp.broadcast_to(logs, (ROWS, ROWS)), 0.0)
        column = jnp.sum(spread, axis=1, keepdims=True)
        hi = column.astype(jnp.bfloat16).astype(jnp.float32)
        rest = column - hi
        mid = rest.astype(jnp.bfloat16).astype(jnp.float32)
        low = rest - mid
        ext = jnp.where(lane == 0, hi, jnp.where(lane == 1, mid, jnp.where(lane == 2, low, 0.0)))
        kx[pl.ds(pl.multiple_of(t * ROWS, ROWS), ROWS), :] = ext.astype(jnp.bfloat16)
        return 0

    lax.fori_loop(0, NDEV, extend, 0)

    def pass_g_on(slot, _):
        half = gb.at[slot, :, step]
        pltpu.make_async_copy(half, half, in_recv.at[slot, 3]).wait()
        forward_g(slot).start()
        return 0

    lax.fori_loop(0, n_slots, pass_g_on, 0)

    for copy in small:
        copy.wait()
    beta = jnp.where(gate_ref[...] == 1, jax.nn.sigmoid(logit_ref[...]), 1.0)
    coef_row = jnp.where(step == 1, beta, 1.0 - beta)
    head_lane = lax.broadcasted_iota(jnp.int32, (1, HEADS), 1)
    ones = jnp.ones((BQ, DH), jnp.bfloat16)

    def do_slot(slot, _):
        h = jnp.where(slot == 0, first_head, second_head)
        coef = jnp.sum(jnp.where(head_lane == h, coef_row, 0.0), axis=1, keepdims=True)
        cols = columns(h)
        for a, buf in enumerate((kb, vb)):
            pltpu.make_async_copy(buf.at[slot], buf.at[slot], in_recv.at[slot, a]).wait()
        forward_g(slot).wait_recv()

        def transpose_keys(t, _):
            rows = pl.ds(pl.multiple_of(t * ROWS, ROWS), ROWS)
            kt[:, rows] = kb[slot, rows, :].astype(jnp.float32).T.astype(jnp.bfloat16)
            dk_acc[rows, :] = jnp.zeros((ROWS, DH), jnp.float32)
            dv_acc[rows, :] = jnp.zeros((ROWS, DH), jnp.float32)
            return 0

        lax.fori_loop(0, NDEV, transpose_keys, 0)

        def send_rows(src_buf, dst_out, a, t):
            rows = pl.ds(pl.multiple_of(t * ROWS, ROWS), ROWS)
            src = src_buf.at[slot, rows]
            dst = dst_out.at[0, :, cols]

            @pl.when(t == me)
            def _():
                pltpu.make_async_copy(src, dst, out_recv.at[a]).start()

            @pl.when(t != me)
            def _():
                pltpu.make_async_remote_copy(
                    src_ref=src, dst_ref=dst, send_sem=out_send.at[slot, a],
                    recv_sem=out_recv.at[a], device_id={"ctx": t}, device_id_type=MESH,
                ).start()

        def unit(b, r_sum):
            q_rows = pl.ds(pl.multiple_of(b * BQ, BQ), BQ)
            q_in = qb.at[slot, q_rows]
            pltpu.make_async_copy(q_in, q_in, q_recv.at[slot, b]).wait()
            g_blk = gb[slot, pl.ds(b * (BQ // ROWS), BQ // ROWS)].reshape(BQ, DH)
            q_ext = jnp.concatenate([qb[slot, q_rows, :], ones], axis=1)

            def pass1(c, top):
                rows = pl.ds(pl.multiple_of(c * CK, CK), CK)
                k_ext = jnp.concatenate([kb[slot, rows, :], kx[rows, :]], axis=1)
                s = lax.dot_general(k_ext, q_ext, NT, preferred_element_type=jnp.float32)
                s_buf[rows, :] = s
                return jnp.maximum(top, jnp.max(s.reshape(CK // 8, 8, BQ), axis=0))

            top = lax.fori_loop(
                0, TOK // CK, pass1, jnp.full((8, BQ), -jnp.inf, jnp.float32)
            )
            top = jnp.max(top, axis=0, keepdims=True)

            def pass2(c, carry):
                l_sum, rd_sum = carry
                rows = pl.ds(pl.multiple_of(c * CK, CK), CK)
                o = lax.dot_general(
                    vb[slot, rows, :], g_blk, NT,
                    preferred_element_type=jnp.float32,
                )
                e = jnp.exp2((s_buf[rows, :] - top) * (SCALE * math.log2(math.e)))
                s_buf[rows, :] = e
                o_buf[rows, :] = o
                l_sum = l_sum + jnp.sum(e.reshape(CK // 8, 8, BQ), axis=0)
                rd_sum = rd_sum + jnp.sum((e * o).reshape(CK // 8, 8, BQ), axis=0)
                return (l_sum, rd_sum)

            zero = jnp.zeros((8, BQ), jnp.float32)
            l_sum, rd_sum = lax.fori_loop(0, TOK // CK, pass2, (zero, zero))
            inv = 1.0 / jnp.sum(l_sum, axis=0, keepdims=True)
            rd = jnp.sum(rd_sum, axis=0, keepdims=True) * inv
            for i in range(BQ // DH):
                r_sum = r_sum + rd[:, i * DH:(i + 1) * DH]

            @pl.when(b == UNITS - 1)
            def _():
                rmine[slot] = r_sum

                def send_r(j, _):
                    pltpu.make_async_remote_copy(
                        src_ref=rmine.at[slot], dst_ref=rb.at[h],
                        send_sem=rb_send.at[slot], recv_sem=rb_recv,
                        device_id={"ctx": (me + j) % NDEV}, device_id_type=MESH,
                    ).start()
                    return 0

                lax.fori_loop(1, NDEV, send_r, 0)
                pltpu.make_async_copy(rmine.at[slot], rb.at[h], rb_recv).start()

            inv = inv * coef
            inv_col = jnp.concatenate(
                [
                    jnp.broadcast_to(inv[:, i * DH:(i + 1) * DH], (DH, DH)).T
                    for i in range(BQ // DH)
                ],
                axis=0,
            )
            g_scaled = (g_blk.astype(jnp.float32) * inv_col).astype(jnp.bfloat16)
            inv_col = inv_col * SCALE
            q_scaled = (qb[slot, q_rows, :].astype(jnp.float32) * inv_col).astype(jnp.bfloat16)

            def pass3(c, _):
                rows = pl.ds(pl.multiple_of(c * CK, CK), CK)
                e = s_buf[rows, :]
                ds = (e * (o_buf[rows, :] - rd)).astype(jnp.bfloat16)
                ds_buf[rows, :] = ds
                dv_acc[rows, :] += jnp.dot(
                    e.astype(jnp.bfloat16), g_scaled, preferred_element_type=jnp.float32
                )
                dk_acc[rows, :] += jnp.dot(ds, q_scaled, preferred_element_type=jnp.float32)
                return 0

            def finish(t, _):
                t = (t // 4) * 4 + (t + me) % 4
                rows = pl.ds(pl.multiple_of(t * ROWS, ROWS), ROWS)
                dks[slot, rows, :] = dk_acc[rows, :].astype(jnp.bfloat16)
                dvs[slot, rows, :] = dv_acc[rows, :].astype(jnp.bfloat16)
                send_rows(dks, dk_out, 1, t)
                send_rows(dvs, dv_out, 2, t)
                return 0

            def pass3_send(c, _):
                far_first = jnp.logical_and(slot == 1, z == 0)
                c = jnp.where(far_first, TOK // CK - 1 - c, c)
                pass3(c, 0)

                @pl.when(b == UNITS - 1)
                def _():
                    lax.fori_loop(c * (CK // ROWS), (c + 1) * (CK // ROWS), finish, 0)

                return 0

            lax.fori_loop(0, TOK // CK, pass3_send, 0)
            dqt = jnp.dot(kt[...], ds_buf[...], preferred_element_type=jnp.float32)
            dqs[slot, q_rows, :] = (dqt.T * inv_col).astype(jnp.bfloat16)

            def send_dq(i, _):
                send_rows(dqs, dq_out, 0, b * (BQ // ROWS) + i)
                return 0

            lax.fori_loop(0, BQ // ROWS, send_dq, 0)
            return r_sum

        lax.fori_loop(0, UNITS, unit, jnp.zeros((1, DH), jnp.float32))
        return 0

    lax.fori_loop(0, n_slots, do_slot, 0)

    pltpu.make_async_copy(rb, rb, rb_recv).wait()
    sums = jnp.sum(rb[...], axis=2)
    diagonal = (
        lax.broadcasted_iota(jnp.int32, (HEADS, DH), 0)
        == lax.broadcasted_iota(jnp.int32, (HEADS, DH), 1)
    )
    rrow[...] = jnp.sum(jnp.where(diagonal, sums, 0.0), axis=0, keepdims=True)
    to_partner = pltpu.make_async_remote_copy(
        src_ref=rrow, dst_ref=rother, send_sem=rp_send, recv_sem=rp_recv,
        device_id={"step": 1 - step}, device_id_type=MESH,
    )
    to_partner.start()

    pltpu.make_async_copy(msb.at[pl.ds(0, NDEV - 1)], msb.at[pl.ds(0, NDEV - 1)], ms_send).wait()

    sent = kb.at[0, pl.ds(0, 3 * ROWS + HALF)]

    def sent_head(h, _):
        @pl.when(owner_of(h, core) != me)
        def _():
            pltpu.make_async_copy(
                sent, sent, in_send.at[h]
            ).wait()

        return 0

    lax.fori_loop(0, HEADS, sent_head, 0)

    def sent_slot(slot, _):
        for a, buf in enumerate((dqs, dks, dvs)):
            part = buf.at[slot, pl.ds(0, TOK - ROWS)]
            pltpu.make_async_copy(part, part, out_send.at[slot, a]).wait()
        part = rb.at[pl.ds(0, NDEV - 1)]
        pltpu.make_async_copy(part, part, rb_send.at[slot]).wait()
        forward_g(slot).wait_send()
        return 0

    lax.fori_loop(0, n_slots, sent_slot, 0)

    to_partner.wait()
    sign = jnp.where(step == 1, 1.0, -1.0).astype(jnp.float32)
    total = (rrow[...] - rother[...]) * sign
    r_out[...] = beta * (1.0 - beta) * total[:, :HEADS] * (1.0 / math.sqrt(TOK))
    for a, out in enumerate((dq_out, dk_out, dv_out)):
        pltpu.make_async_copy(out, out, out_recv.at[a]).wait()


def hand_over(dq_in, dk_in, dv_in, r_in, dq_out, dk_out, dv_out, r_out, sems):
    copies = [pltpu.make_async_copy(r_in, r_out, sems.at[0])]
    for a, (src, dst) in enumerate(((dq_in, dq_out), (dk_in, dk_out), (dv_in, dv_out))):
        for i in range(2):
            rows = pl.ds(i * HALF, HALF)
            copies.append(
                pltpu.make_async_copy(src.at[0, rows], dst.at[0, rows], sems.at[1 + 2 * a + i])
            )
    for copy in copies:
        copy.start()
    for copy in copies:
        copy.wait()


def body(queries, keys, values, cotangent, merge_sizes, router_logits, gate_plan):
    shape = queries.shape
    bf16, f32 = jnp.bfloat16, jnp.float32
    anywhere = pl.BlockSpec(memory_space=pl.ANY)
    whole = pl.BlockSpec(memory_space=pltpu.VMEM)
    dma = pltpu.SemaphoreType.DMA
    dq, dk, dv, r = pl.pallas_call(
        kernel,
        out_shape=[
            pltpu.VMEM(shape, bf16),
            pltpu.VMEM(shape, bf16),
            pltpu.VMEM(shape, bf16),
            pltpu.VMEM((1, HEADS), f32),
        ],
        in_specs=[anywhere] * 7,
        out_specs=[whole] * 4,
        scratch_shapes=[
            pltpu.VMEM((2, TOK, DH), bf16),
            pltpu.VMEM((2, TOK, DH), bf16),
            pltpu.VMEM((2, TOK, DH), bf16),
            pltpu.VMEM((2, NDEV, 2, HALF, DH), bf16),
            pltpu.VMEM((NDEV, 1, ROWS), jnp.int32),
            pltpu.VMEM((TOK, DH), bf16),
            pltpu.VMEM((DH, TOK), bf16),
            pltpu.VMEM((TOK, BQ), f32),
            pltpu.VMEM((TOK, BQ), f32),
            pltpu.VMEM((TOK, BQ), bf16),
            pltpu.VMEM((TOK, DH), f32),
            pltpu.VMEM((TOK, DH), f32),
            pltpu.VMEM((2, TOK, DH), bf16),
            pltpu.VMEM((2, TOK, DH), bf16),
            pltpu.VMEM((2, TOK, DH), bf16),
            pltpu.VMEM((2, 1, DH), f32),
            pltpu.VMEM((HEADS, 1, DH), f32),
            pltpu.VMEM((1, DH), f32),
            pltpu.VMEM((1, DH), f32),
            pltpu.VMEM((1, HEADS), f32),
            pltpu.VMEM((1, HEADS), jnp.int32),
            dma((HEADS,)),
            dma((2, 4)),
            dma((2, UNITS)),
            dma((2,)), dma((2,)),
            dma, dma,
            dma((2, 3)),
            dma((3,)),
            dma, dma,
            dma((2,)), dma,
            dma((2,)),
        ],
        compiler_params=pltpu.CompilerParams(
            collective_id=0, has_side_effects=True, vmem_limit_bytes=60 * 1024 * 1024
        ),
        cost_estimate=pl.CostEstimate(
            flops=7_000_000_000, bytes_accessed=5_000_000, transcendentals=5_000_000
        ),
    )(
        router_logits.reshape(1, HEADS), gate_plan.reshape(1, HEADS),
        queries, keys, values, cotangent, merge_sizes.reshape(1, ROWS),
    )
    held = [pltpu.with_memory_space_constraint(a, pltpu.VMEM) for a in (dq, dk, dv, r)]
    dq, dk, dv, r = pl.pallas_call(
        hand_over,
        out_shape=[jax.ShapeDtypeStruct(shape, bf16)] * 3
        + [jax.ShapeDtypeStruct((1, HEADS), f32)],
        in_specs=[whole] * 4,
        out_specs=[anywhere] * 4,
        scratch_shapes=[dma((7,))],
        compiler_params=pltpu.CompilerParams(vmem_limit_bytes=60 * 1024 * 1024),
    )(*held)
    return (dq, dk, dv, r.reshape(HEADS))


def solution(mesh):
    return jax.shard_map(
        body,
        mesh=mesh,
        in_specs=(
            P("step", ("grp", "ctx"), None),
            P("step", ("grp", "ctx"), None),
            P("step", ("grp", "ctx"), None),
            P(("grp", "ctx"), None),
            P(("grp", "ctx")),
            P(),
            P(),
        ),
        out_specs=(
            P("step", ("grp", "ctx"), None),
            P("step", ("grp", "ctx"), None),
            P("step", ("grp", "ctx"), None),
            P("grp"),
        ),
        check_vma=False,
    )
```
